512 devices in a mesh: wide: 128 (over z, y, core), narrow: 4 (over x).
Axes of the slice: x: 4, y: 8, z: 8, core: 2. Of those that a mesh axis runs over, the one named last changes fastest.
Arguments:
- features: bfloat16 [32768, 512], P('wide', 'narrow'), may hold values from -6 to 6
- tile_blocks: bfloat16 [128, 4, 48, 128, 128], P('wide', 'narrow'), may hold values from -0.078125 to 0.078125
- tile_rows: int32 [128, 4, 48], P('wide', 'narrow'), may hold values from 0 to 1
- tile_cols: int32 [128, 4, 48], P('wide', 'narrow'), may hold values from 0 to 63, as said below
- tile_count: int32 [128, 4], P('wide', 'narrow'), may hold values from 12 to 48, as said below
- neighbor_weight: bfloat16 [512, 512], P('narrow'), may hold values from -0.25 to 0.25
- root_weight: bfloat16 [512, 512], P('narrow'), may hold values from -0.25 to 0.25
- output_weight: bfloat16 [512, 512], replicated, may hold values from -0.25 to 0.25
- cotangent: bfloat16 [32768, 512], P('wide'), may hold values from -0.078125 to 0.078125
Outputs:
- layer_output: bfloat16 [32768, 512], P('wide', 'narrow')
- neighbor_grad: float32 [512, 512], P('narrow')
- root_grad: float32 [512, 512], P('narrow')
- output_grad: float32 [512, 512], P(None, 'narrow')
The draws below stay inside these ranges and needn't reach their ends.
Inputs may be any that keep to these rules, and one draw needn't show every extreme that they name: `tile_count`: slots at or past a device's count hold no tiles and are ignored; the largest count is 48 on some device in every draw, the smallest max(1, 12) on another. `tile_cols`: positions may repeat; repeated tiles add. Slot 0 of every device of row block b names the column tile that holds the nodes of row block b + 128 // 2 (counted round).
All inputs are finite; a program needn't handle non-finite values.
Results may differ from the reference program's by a relative error of at most 0.015.
Values may be sent and summed in bfloat16 or wider, within the bound.
No kernel may reach another device: no remote copies, remote signals or barrier semaphores. Data moves between devices by JAX's collectives and lax.ppermute only.
A program may use at most 64 MiB of HBM per device.

```python
import jax
import jax.numpy as jnp
from jax import lax

H = 512
TILE = 128
TROWS = 2
TCAP = 48
ROWS = 256
NODES = 32768
QUARTER = 64
COLTILES = 64
N_WIDE = 128
N_NARROW = 4


def draw_tile_count(key, part):
    key = jax.random.fold_in(key, 7)
    first_key, second_key, third_key = jax.random.split(key, 3)
    total = N_WIDE * N_NARROW
    lowest = max(1, TCAP // 4)
    spread = jax.random.randint(first_key, (total,), 0, 17)
    counts = lowest + spread * spread * (TCAP - lowest) // 256
    busiest = jax.random.randint(second_key, (), 0, total)
    quietest = (busiest + 1 + jax.random.randint(third_key, (), 0, total - 1)) % total
    places = jnp.arange(total)
    counts = jnp.where(places == busiest, TCAP, jnp.where(places == quietest, lowest, counts))
    return counts.reshape(N_WIDE, N_NARROW).astype(jnp.int32)


def draw_tile_cols(key, part):
    key = jax.random.fold_in(key, 11)
    columns = jax.random.randint(key, (N_WIDE, N_NARROW, TCAP), 0, COLTILES)
    across = (jnp.arange(N_WIDE, dtype=jnp.int32) + N_WIDE // 2) % N_WIDE
    holding = across * QUARTER // TILE
    columns = columns.at[:, :, 0].set(jnp.broadcast_to(holding[:, None], (N_WIDE, N_NARROW)))
    return columns.astype(jnp.int32)


def touch_ends(entries, rng, least, high):
    index_at = [jax.random.randint(jax.random.fold_in(rng, axis), (), 0, length) for axis, length in enumerate(entries.shape)]
    main_axis = entries.shape.index(max(entries.shape))
    beside = index_at[:main_axis] + [(index_at[main_axis] + 1) % entries.shape[main_axis]] + index_at[main_axis + 1:]
    return entries.at[tuple(index_at)].set(least).at[tuple(beside)].set(high)


def levels(key, extent, cuts, smallest, largest):
    gain = 1.0
    for position, blocks in cuts:
        draws = jax.random.uniform(jax.random.fold_in(jax.random.fold_in(key, 6), position), (blocks,), jnp.float32, smallest / len(cuts), largest / len(cuts))
        gain = gain * jnp.repeat(jnp.exp(draws), extent[position] // blocks).reshape((-1,) + (1,) * (len(extent) - 1 - position))
    return gain


def centred(own_key, shape, scale, bound, cuts=(), kind=jnp.bfloat16):
    entries = scale * jax.random.normal(own_key, shape, jnp.float32)
    if cuts:
        entries = entries * levels(own_key, shape, cuts, -0.22, 0.18)
    return jnp.clip(entries, -bound, bound).astype(kind)


def setup_inputs(seed: int = 0) -> dict:
    keys = jax.random.split(jax.random.key(seed), 10)
    return {
        "features": centred(keys[0], (NODES, H), 1.0, 6.0, ((0, 128), (1, 4))),
        "tile_blocks": centred(keys[1], (N_WIDE, N_NARROW, TCAP, TILE, TILE), (256 * TCAP // TROWS) ** -0.5, 0.078125, ((0, 128), (1, 4))),
        "tile_rows": touch_ends(jax.random.randint(keys[2], (N_WIDE, N_NARROW, TCAP), 0, TROWS), jax.random.fold_in(keys[2], 1), 0, TROWS - 1).astype(jnp.int32),
        "tile_cols": draw_tile_cols(jax.random.fold_in(keys[9], 71), 0),
        "tile_count": draw_tile_count(jax.random.fold_in(keys[9], 71), 0),
        "neighbor_weight": centred(keys[5], (H, H), H ** -0.5, 0.25, ((0, 4),)),
        "root_weight": centred(keys[6], (H, H), H ** -0.5, 0.25, ((0, 4),)),
        "output_weight": centred(keys[7], (H, H), H ** -0.5, 0.25),
        "cotangent": centred(keys[8], (NODES, H), (NODES ** -0.5), 0.078125, ((0, 128),)),
    }


def aggregate(features, tile_blocks, tile_rows, tile_cols, tile_count):
    groups = features.reshape(N_WIDE, N_NARROW, QUARTER, H).transpose(1, 0, 2, 3)
    groups = groups.reshape(N_NARROW, COLTILES, TILE, H)
    slot_ids = jnp.arange(TCAP, dtype=jnp.int32)
    group_ids = jnp.arange(N_NARROW, dtype=jnp.int32)
    row_ids = jnp.arange(TROWS, dtype=jnp.int32)

    def one_block(inputs):
        block_tiles, block_rows, block_cols, block_count = inputs
        alive = (slot_ids[None, :] < block_count[:, None]).astype(jnp.float32)
        picked = groups[group_ids[:, None], block_cols]
        product = jnp.einsum("gtij,gtjh->gtih", block_tiles.astype(jnp.float32), picked.astype(jnp.float32))
        placing = alive[:, :, None] * (block_rows[:, :, None] == row_ids[None, None, :]).astype(jnp.float32)
        return jnp.einsum("gtr,gtih->rih", placing, product).reshape(ROWS, H)

    summed = lax.map(one_block, (tile_blocks, tile_rows, tile_cols, tile_count))
    return summed.reshape(NODES, H).astype(jnp.bfloat16)


def reference(features, tile_blocks, tile_rows, tile_cols, tile_count, neighbor_weight, root_weight, output_weight, cotangent):
    agg = aggregate(features, tile_blocks, tile_rows, tile_cols, tile_count)
    pre = jnp.dot(agg, neighbor_weight, preferred_element_type=jnp.float32) + jnp.dot(features, root_weight, preferred_element_type=jnp.float32)
    hidden = jax.nn.silu(pre).astype(jnp.bfloat16)
    layer_output = (features.astype(jnp.float32) + jnp.dot(hidden, output_weight, preferred_element_type=jnp.float32)).astype(jnp.bfloat16)
    hidden_grad = jnp.dot(cotangent, output_weight.T, preferred_element_type=jnp.float32)
    sigmoid_pre = jax.nn.sigmoid(pre)
    pre_grad = (hidden_grad * sigmoid_pre * (1.0 + pre * (1.0 - sigmoid_pre))).astype(jnp.bfloat16)
    neighbor_grad = jnp.dot(agg.T, pre_grad, preferred_element_type=jnp.float32)
    root_grad = jnp.dot(features.T, pre_grad, preferred_element_type=jnp.float32)
    output_grad = jnp.dot(hidden.T, cotangent, preferred_element_type=jnp.float32)
    return layer_output, neighbor_grad, root_grad, output_grad
```

```python
import functools

import jax
import jax.numpy as jnp
from jax import lax
from jax.experimental import pallas as pl
from jax.experimental.pallas import tpu as pltpu
from jax.sharding import PartitionSpec as P

AXES = ("wide", "narrow")
NZ, NY, NC, NN = 8, 8, 2, 4
VMEM = pl.BlockSpec(memory_space=pltpu.VMEM)
SMEM = pl.BlockSpec(memory_space=pltpu.SMEM)
BIG = pltpu.CompilerParams(vmem_limit_bytes=48 * 1024 * 1024)
F32, BF16 = jnp.float32, jnp.bfloat16


def places():
    for z in range(NZ):
        for y in range(NY):
            for c in range(NC):
                for n in range(NN):
                    yield z, y, c, n


def device(z, y, c, n):
    return ((z * NY + y) * NC + c) * NN + n


def groups(key):
    found = {}
    for place in places():
        found.setdefault(key(*place), []).append(device(*place))
    return list(found.values())


FIRST = groups(lambda z, y, c, n: (0, y) if c == 0 else (1, z))
SECOND = groups(lambda z, y, c, n: (c, z, n) if c == 0 else (c, y, n))
OVER_X = groups(lambda z, y, c, n: (z, y, c))
OVER_ZC = groups(lambda z, y, c, n: (y, n))
OVER_Y = groups(lambda z, y, c, n: (z, c, n))
OTHER_CORE = [(device(z, y, c, n), device(z, y, 1 - c, n)) for z, y, c, n in places()]


def exchange(pieces, groups_):
    return lax.all_to_all(pieces, AXES, 0, 0, axis_index_groups=groups_, tiled=True)


def share(piece, count, groups_):
    return exchange(jnp.broadcast_to(piece[None], (count, *piece.shape)), groups_)


def swap_cores(value):
    return lax.ppermute(value, AXES, OTHER_CORE)


def place_kernel(s_ref, own_ref, other_ref, lo_ref, lt_ref):
    slots = own_ref.shape[0]
    core = s_ref[4 * slots + 2]
    first = core == 0
    low = lax.broadcasted_iota(jnp.int32, own_ref.shape[1:], 1) < own_ref.shape[2] // 2
    half = own_ref.shape[2] // 2
    for block, (t_ref, l_ref) in enumerate(((own_ref, lo_ref), (other_ref, lt_ref))):
        base = 2 * slots * block
        count = s_ref[4 * slots + block]

        def one_pair(p, carry, t_ref=t_ref, l_ref=l_ref, base=base, count=count):
            a = t_ref[2 * p].astype(F32)
            b = t_ref[2 * p + 1].astype(F32)
            moved = pltpu.roll(jnp.where(first, b, a), half, 1)
            both = jnp.where(low, jnp.where(first, a, moved), jnp.where(first, moved, b))
            row_a, row_b = s_ref[base + 2 * p], s_ref[base + 2 * p + 1]
            row_a = jnp.where(2 * p < count, row_a, -1)
            row_b = jnp.where(2 * p + 1 < count, row_b, -1)
            rows = jnp.where(low, row_a, row_b)
            side = both.shape[0]
            for r in range(2):
                l_ref[p, r * side:(r + 1) * side, :] = jnp.where(rows == r, both, 0.0).astype(BF16)
            return carry

        lax.fori_loop(0, slots // 2, one_pair, 0)


def sum_kernel(s_ref, lo_ref, lt_ref, g_ref, po_ref, pt_ref, acc):
    slots = 2 * lo_ref.shape[0]
    step = 8
    for block, (l_ref, p_ref) in enumerate(((lo_ref, po_ref), (lt_ref, pt_ref))):
        base = 2 * slots * block + slots
        count = s_ref[4 * slots + block]
        acc[...] = jnp.zeros_like(acc)

        def one_turn(i, carry, l_ref=l_ref, base=base):
            left = jnp.concatenate([l_ref[i * (step // 2) + k] for k in range(step // 2)], axis=1)
            spots = [s_ref[base + i * step + k] * NN for k in range(step)]
            right = jnp.concatenate(
                [jnp.concatenate([g_ref[spot + n] for spot in spots], axis=0) for n in range(NN)],
                axis=1,
            )
            acc[...] += jnp.dot(left, right, preferred_element_type=F32)
            return carry

        lax.fori_loop(0, (count + step - 1) // step, one_turn, 0)
        p_ref[...] = acc[...].astype(p_ref.dtype)


def early_kernel(w_ref, cot_ref, ow_ref, root_ref, hg_ref):
    width = w_ref.shape[2]
    side = width // NN
    quarter = w_ref.shape[1] - 2 * side
    root_weight = jnp.concatenate([w_ref[j, side:2 * side, :] for j in range(NN)], axis=0)
    for q in range(NN):
        rows = jnp.concatenate(
            [w_ref[j, 2 * side:, q * side:(q + 1) * side] for j in range(NN)], axis=1
        )
        root_ref[q * quarter:(q + 1) * quarter, :] = jnp.dot(
            rows, root_weight, preferred_element_type=F32
        )
    hg_ref[...] = lax.dot_general(
        cot_ref[...], ow_ref[...], (((1,), (1,)), ((), ())), preferred_element_type=F32
    )


def dense_kernel(n_ref, a_ref, w_ref, root_ref, hg_ref, f_ref, cot_ref, ow_ref, out_ref, g_ref, agg_ref):
    side = f_ref.shape[1]
    mine = pl.ds(pl.multiple_of(n_ref[0] * side, side), side)
    agg = a_ref[0].astype(F32)
    for j in range(1, NN):
        agg = agg + a_ref[j].astype(F32)
    agg = agg.astype(BF16)
    agg_ref[...] = agg
    weight = jnp.concatenate([w_ref[j, :side, :] for j in range(NN)], axis=0)
    pre = jnp.dot(agg, weight, preferred_element_type=F32) + root_ref[...]
    s = jax.nn.sigmoid(pre)
    hidden = (pre * s).astype(BF16)
    pre_grad = (hg_ref[...] * s * (1.0 + pre * (1.0 - s))).astype(BF16)
    over_rows = (((0,), (0,)), ((), ()))
    parts = (
        lax.dot_general(agg_ref[:, mine], pre_grad, over_rows, preferred_element_type=F32),
        lax.dot_general(f_ref[...], pre_grad, over_rows, preferred_element_type=F32),
    )
    for k, part in enumerate(parts):
        for j in range(NN):
            g_ref[k * NN + j] = part[:, j * side:(j + 1) * side].astype(BF16)
    part = lax.dot_general(hidden, cot_ref[:, mine], over_rows, preferred_element_type=F32)
    for j in range(NN):
        g_ref[2 * NN + j] = part[j * side:(j + 1) * side, :].astype(BF16)
    out_ref[...] = (
        f_ref[...].astype(F32) + jnp.dot(hidden, ow_ref[:, mine], preferred_element_type=F32)
    ).astype(BF16)


def total(pieces):
    return jnp.sum(pieces.astype(F32), axis=0).astype(BF16)


def per_device(
    features,
    tile_blocks,
    tile_rows,
    tile_cols,
    tile_count,
    neighbor_weight,
    root_weight,
    output_weight,
    cotangent,
):
    rows, side = features.shape
    quarter = rows // NN
    slots = tile_rows.shape[-1]
    core = lax.rem(lax.axis_index("wide"), NC)
    narrow = lax.axis_index("narrow")

    pieces = jnp.broadcast_to(
        features.reshape(1, NN, quarter, side), (NZ, NN, quarter, side)
    ).reshape(NZ * NN, quarter, side)
    line = exchange(pieces, FIRST)
    weights = jnp.concatenate(
        [
            neighbor_weight,
            root_weight,
            features.reshape(NN, quarter, side).swapaxes(0, 1).reshape(quarter, NN * side),
        ],
        axis=0,
    )
    tiles = tile_blocks[0, 0]
    numbers = jnp.concatenate([tile_rows[0, 0], tile_cols[0, 0], tile_count[0]])
    line, weights, tiles, numbers = lax.optimization_barrier((line, weights, tiles, numbers))
    plane = lax.all_gather(line, AXES, axis_index_groups=SECOND, axis=0, tiled=True)

    other_tiles = swap_cores(tiles)
    other_numbers = swap_cores(numbers)
    all_weights = share(weights, NN, OVER_X)

    def spot(cols):
        return jnp.where(core == 0, (cols % NY) * NZ + cols // NY, cols)

    scalars = jnp.concatenate(
        [
            numbers[:slots],
            spot(numbers[slots:2 * slots]),
            other_numbers[:slots],
            spot(other_numbers[slots:2 * slots]),
            numbers[2 * slots:],
            other_numbers[2 * slots:],
            core[None],
        ]
    ).astype(jnp.int32)
    placed = jax.ShapeDtypeStruct((slots // 2, rows, tiles.shape[-1]), BF16)
    left_own, left_other = pl.pallas_call(
        place_kernel,
        out_shape=(placed, placed),
        in_specs=[SMEM, VMEM, VMEM],
        out_specs=(VMEM, VMEM),
        compiler_params=BIG,
        cost_estimate=pl.CostEstimate(flops=10**6, bytes_accessed=6 * 10**6, transcendentals=0),
        name="place",
    )(scalars, tiles, other_tiles)
    width = NN * side
    whole = jax.ShapeDtypeStruct((rows, width), F32)
    root_part, hidden_grad = pl.pallas_call(
        early_kernel,
        out_shape=(whole, whole),
        in_specs=[VMEM, VMEM, VMEM],
        out_specs=(VMEM, VMEM),
        compiler_params=BIG,
        cost_estimate=pl.CostEstimate(
            flops=4 * rows * width * width, bytes_accessed=4 * 10**6, transcendentals=0
        ),
        name="early",
    )(all_weights.reshape(NN, *weights.shape), cotangent, output_weight)

    part_own, part_other = pl.pallas_call(
        sum_kernel,
        out_shape=(whole, jax.ShapeDtypeStruct((rows, width), BF16)),
        in_specs=[SMEM, VMEM, VMEM, VMEM],
        out_specs=(VMEM, VMEM),
        scratch_shapes=[pltpu.VMEM((rows, width), F32)],
        compiler_params=BIG,
        cost_estimate=pl.CostEstimate(
            flops=2 * slots * rows * quarter * width * 2, bytes_accessed=8 * 10**6, transcendentals=0
        ),
        name="sum",
    )(scalars, left_own, left_other, plane)
    block_part = (part_own + swap_cores(part_other).astype(F32)).astype(BF16)
    parts = share(block_part, NN, OVER_X)

    layer_output, grads = pl.pallas_call(
        dense_kernel,
        out_shape=(
            jax.ShapeDtypeStruct((rows, side), BF16),
            jax.ShapeDtypeStruct((3 * NN, side, side), BF16),
        ),
        in_specs=[SMEM] + [VMEM] * 7,
        out_specs=(VMEM, VMEM),
        scratch_shapes=[pltpu.VMEM((rows, width), BF16)],
        compiler_params=BIG,
        cost_estimate=pl.CostEstimate(
            flops=4 * rows * width * width, bytes_accessed=5 * 10**6, transcendentals=rows * width
        ),
        name="dense",
    )(
        narrow[None],
        parts.reshape(NN, rows, width),
        all_weights.reshape(NN, *weights.shape),
        root_part,
        hidden_grad,
        features,
        cotangent,
        output_weight,
    )

    chunk = 3 * NN * side // (NZ * NC)
    summed = total(exchange(grads.reshape(NZ * NC, chunk, side), OVER_ZC))
    summed = total(share(summed, NY, OVER_Y))
    full = share(summed, NZ * NC, OVER_ZC).reshape(3, NN, side, side).astype(F32)
    neighbor_grad, root_grad = (
        full[k].transpose(1, 0, 2).reshape(side, width) for k in range(2)
    )
    output_grad = full[2].reshape(width, side)
    return layer_output, neighbor_grad, root_grad, output_grad


def solution(mesh):
    return jax.shard_map(
        per_device,
        mesh=mesh,
        in_specs=(
            P("wide", "narrow"),
            P("wide", "narrow", None, None, None),
            P("wide", "narrow", None),
            P("wide", "narrow", None),
            P("wide", "narrow"),
            P("narrow", None),
            P("narrow", None),
            P(),
            P("wide", None),
        ),
        out_specs=(P("wide", "narrow"), P("narrow", None), P("narrow", None), P(None, "narrow")),
        check_vma=False,
    )
```

```python
import jax
import jax.numpy as jnp
from jax import lax
from jax.experimental import pallas as pl
from jax.experimental.pallas import tpu as pltpu
from jax.sharding import PartitionSpec as P

AXES = ("wide", "narrow")
NZ, NY, NC, NN = 8, 8, 2, 4
STEP = 8
VMEM = pl.BlockSpec(memory_space=pltpu.VMEM)
SMEM = pl.BlockSpec(memory_space=pltpu.SMEM)
ANY = pl.BlockSpec(memory_space=pl.ANY)
F32, BF16, I32 = jnp.float32, jnp.bfloat16, jnp.int32
NEAR = (0, 7, 1, 6, 2)
FAR = (5, 3, 4)


def places():
    for z in range(NZ):
        for y in range(NY):
            for c in range(NC):
                for n in range(NN):
                    yield z, y, c, n


def device(z, y, c, n):
    return ((z * NY + y) * NC + c) * NN + n


def groups(key):
    found = {}
    for place in places():
        found.setdefault(key(*place), []).append(device(*place))
    return list(found.values())


FIRST = groups(lambda z, y, c, n: (0, y) if c == 0 else (1, z))
OVER_X = groups(lambda z, y, c, n: (z, y, c))
OVER_ZC = groups(lambda z, y, c, n: (y, n))
OVER_Y = groups(lambda z, y, c, n: (z, c, n))
OTHER_CORE = [(device(z, y, c, n), device(z, y, 1 - c, n)) for z, y, c, n in places()]


def exchange(pieces, groups_):
    return lax.all_to_all(pieces, AXES, 0, 0, axis_index_groups=groups_, tiled=True)


def swap_cores(value):
    return lax.ppermute(value, AXES, OTHER_CORE)


def pass_on(value, hops):
    pairs = []
    for z, y, c, n in places():
        to = (z, (y + hops) % NY, c, n) if c == 0 else ((z + hops) % NZ, y, c, n)
        pairs.append((device(z, y, c, n), device(*to)))
    return lax.ppermute(value, AXES, pairs)


def call(kernel, name, out_shape, in_specs, out_specs, scratch, vmem, flops, size, *args):
    return pl.pallas_call(
        kernel,
        out_shape=out_shape,
        in_specs=in_specs,
        out_specs=out_specs,
        scratch_shapes=scratch,
        compiler_params=pltpu.CompilerParams(vmem_limit_bytes=vmem << 20),
        cost_estimate=pl.CostEstimate(flops=flops, bytes_accessed=size, transcendentals=0),
        name=name,
    )(*args)


def place_kernel(where_ref, own_n_ref, other_n_ref, own_ref, other_ref, lo_ref, lt_ref, meta_ref, order):
    slots, half = own_ref.shape[0], own_ref.shape[2] // 2
    side = own_ref.shape[1]
    room = meta_ref.shape[1] - 2
    first = where_ref[0] == 0
    here = where_ref[1]
    low = lax.broadcasted_iota(I32, own_ref.shape[1:], 1) < half
    for block, (n_ref, t_ref, l_ref) in enumerate(
        ((own_n_ref, own_ref, lo_ref), (other_n_ref, other_ref, lt_ref))
    ):
        count = n_ref[2 * slots]

        def clear(k, carry, block=block):
            order[k] = -1
            meta_ref[block, k] = 0
            return carry

        lax.fori_loop(0, room, clear, 0)

        def looked_up(s, n_ref=n_ref):
            col = n_ref[slots + s]
            z, y = lax.shift_right_logical(col, 3), lax.bitwise_and(col, 7)
            ring = jnp.where(first, y, z)
            inner = jnp.where(first, z, y)
            away = lax.bitwise_and(ring - here + 8, 7)
            return away, inner

        def tally(s, near):
            away, _ = looked_up(s)
            return near + jnp.where((away >= 3) & (away <= 5), 0, 1)

        near = lax.fori_loop(0, count, tally, 0)
        near_turns = lax.shift_right_logical(near + STEP - 1, 3)
        far_turns = lax.shift_right_logical(count - near + STEP - 1, 3)
        meta_ref[block, room] = near_turns
        meta_ref[block, room + 1] = near_turns + far_turns

        def assign(s, carry, block=block):
            near_at, far_at = carry
            away, inner = looked_up(s)
            far = (away >= 3) & (away <= 5)
            base = jnp.int32(0)
            for among in (NEAR, FAR):
                for k, distance in enumerate(among):
                    base = jnp.where(away == distance, k, base)
            at = jnp.where(far, far_at, near_at)
            order[at] = s
            meta_ref[block, at] = base * (NZ * NN) + inner * NN
            step = jnp.where(far, 1, 0)
            return near_at + 1 - step, far_at + step

        lax.fori_loop(0, count, assign, (0, near_turns * STEP))

        def one_pair(p, carry, n_ref=n_ref, t_ref=t_ref, l_ref=l_ref):
            slot_a, slot_b = order[2 * p], order[2 * p + 1]
            at_a, at_b = jnp.maximum(slot_a, 0), jnp.maximum(slot_b, 0)
            a, b = t_ref[at_a].astype(F32), t_ref[at_b].astype(F32)
            moved = pltpu.roll(jnp.where(first, b, a), half, 1)
            both = jnp.where(low, jnp.where(first, a, moved), jnp.where(first, moved, b))
            row_a = jnp.where(slot_a >= 0, n_ref[at_a], -1)
            row_b = jnp.where(slot_b >= 0, n_ref[at_b], -1)
            rows = jnp.where(low, row_a, row_b)
            for r in range(2):
                l_ref[p, r * side:(r + 1) * side, :] = jnp.where(rows == r, both, 0.0).astype(BF16)
            return carry

        lax.fori_loop(0, (near_turns + far_turns) * (STEP // 2), one_pair, 0)


def add_turns(meta_ref, block, first_turn, last_turn, l_ref, blocks, acc):
    def one_turn(i, carry):
        left = jnp.concatenate([l_ref[i * (STEP // 2) + k] for k in range(STEP // 2)], axis=1)
        spots = [meta_ref[block, i * STEP + k] for k in range(STEP)]
        right = jnp.concatenate(
            [jnp.concatenate([blocks[spot + n] for spot in spots], axis=0) for n in range(NN)],
            axis=1,
        )
        acc[...] += jnp.dot(left, right, preferred_element_type=F32)
        return carry

    lax.fori_loop(first_turn, last_turn, one_turn, 0)


def bring(refs, blocks, sems):
    copies, at = [], 0
    for k, ref in enumerate(refs):
        copies.append(
            pltpu.make_async_copy(ref, blocks.at[pl.ds(at, ref.shape[0])], sems.at[k])
        )
        at += ref.shape[0]
    for copy in copies:
        copy.start()
    return copies


def near_kernel(meta_ref, lo_ref, lt_ref, *refs):
    *given, po_ref, pt_ref, blocks, sems = refs
    room = meta_ref.shape[1] - 2
    copies = bring(given, blocks, sems)
    po_ref[...] = jnp.zeros_like(po_ref)
    pt_ref[...] = jnp.zeros_like(pt_ref)
    for copy in copies:
        copy.wait()
    add_turns(meta_ref, 1, 0, meta_ref[1, room], lt_ref, blocks, pt_ref)
    add_turns(meta_ref, 0, 0, meta_ref[0, room], lo_ref, blocks, po_ref)


def far_kernel(meta_ref, lo_ref, lt_ref, no_ref, nt_ref, *refs):
    *given, po_ref, pt_ref, acc, blocks, sems = refs
    room = meta_ref.shape[1] - 2
    copies = bring(given, blocks, sems)
    acc[...] = nt_ref[...]
    po_ref[...] = no_ref[...]
    for copy in copies:
        copy.wait()
    add_turns(meta_ref, 1, meta_ref[1, room], meta_ref[1, room + 1], lt_ref, blocks, acc)
    pt_ref[...] = acc[...].astype(BF16)
    add_turns(meta_ref, 0, meta_ref[0, room], meta_ref[0, room + 1], lo_ref, blocks, po_ref)


def join_kernel(own_ref, came_ref, out_ref):
    joined = (own_ref[...] + came_ref[...].astype(F32)).astype(BF16)
    for j in range(out_ref.shape[0]):
        out_ref[j] = joined


def total_kernel(in_ref, out_ref):
    summed = in_ref[0].astype(F32)
    for j in range(1, in_ref.shape[0]):
        summed = summed + in_ref[j].astype(F32)
    summed = summed.astype(BF16)
    for j in range(out_ref.shape[0]):
        out_ref[j] = summed


def last_kernel(in_ref, neighbor_ref, root_ref, output_ref):
    side = in_ref.shape[1]
    for j in range(NN):
        neighbor_ref[:, j * side:(j + 1) * side] = in_ref[j].astype(F32)
        root_ref[:, j * side:(j + 1) * side] = in_ref[NN + j].astype(F32)
        output_ref[j * side:(j + 1) * side, :] = in_ref[2 * NN + j].astype(F32)


def dense_kernel(n_ref, a_ref, w_ref, f_ref, cot_ref, ow_ref, out_ref, g_ref, agg_ref):
    side = f_ref.shape[1]
    quarter = w_ref.shape[1] - 2 * side
    mine = pl.ds(pl.multiple_of(n_ref[0] * side, side), side)
    root_weight = jnp.concatenate([w_ref[j, side:2 * side, :] for j in range(NN)], axis=0)
    neighbor_weight = jnp.concatenate([w_ref[j, :side, :] for j in range(NN)], axis=0)
    rows = jnp.concatenate(
        [
            jnp.concatenate(
                [w_ref[j, 2 * side:, q * side:(q + 1) * side] for j in range(NN)], axis=1
            )
            for q in range(NN)
        ],
        axis=0,
    )
    hidden_grad = lax.dot_general(
        cot_ref[...], ow_ref[...], (((1,), (1,)), ((), ())), preferred_element_type=F32
    )
    agg = a_ref[0].astype(F32)
    for j in range(1, NN):
        agg = agg + a_ref[j].astype(F32)
    agg = agg.astype(BF16)
    agg_ref[...] = agg
    pre = jnp.dot(agg, neighbor_weight, preferred_element_type=F32) + jnp.dot(
        rows, root_weight, preferred_element_type=F32
    )
    s = jax.nn.sigmoid(pre)
    hidden = (pre * s).astype(BF16)
    pre_grad = (hidden_grad * s * (1.0 + pre * (1.0 - s))).astype(BF16)
    over_rows = (((0,), (0,)), ((), ()))
    parts = (
        lax.dot_general(agg_ref[:, mine], pre_grad, over_rows, preferred_element_type=F32),
        lax.dot_general(f_ref[...], pre_grad, over_rows, preferred_element_type=F32),
    )
    for k, part in enumerate(parts):
        for j in range(NN):
            g_ref[k * NN + j] = part[:, j * side:(j + 1) * side].astype(BF16)
    part = lax.dot_general(hidden, cot_ref[:, mine], over_rows, preferred_element_type=F32)
    for j in range(NN):
        g_ref[2 * NN + j] = part[j * side:(j + 1) * side, :].astype(BF16)
    out_ref[...] = (
        f_ref[...].astype(F32) + jnp.dot(hidden, ow_ref[:, mine], preferred_element_type=F32)
    ).astype(BF16)


def per_device(
    features,
    tile_blocks,
    tile_rows,
    tile_cols,
    tile_count,
    neighbor_weight,
    root_weight,
    output_weight,
    cotangent,
):
    rows, side = features.shape
    width = NN * side
    quarter = rows // NN
    slots = tile_rows.shape[-1]
    wide = lax.axis_index("wide")
    narrow = lax.axis_index("narrow").astype(I32)
    core = wide % NC
    here = jnp.where(core == 0, (wide // NC) % NY, wide // (NC * NY))

    tiles = tile_blocks[0, 0]
    numbers = jnp.concatenate([tile_rows[0, 0], tile_cols[0, 0], tile_count[0]])
    other_tiles = swap_cores(tiles)
    other_numbers = swap_cores(numbers)

    pieces = jnp.broadcast_to(
        features.reshape(1, NN, quarter, side), (NZ, NN, quarter, side)
    ).reshape(NZ * NN, quarter, side)
    line = exchange(pieces, FIRST)

    turns = (slots + 2 * STEP - 2) // STEP
    placed = jax.ShapeDtypeStruct((turns * STEP // 2, rows, side), BF16)
    left_own, left_other, meta = call(
        place_kernel,
        "place",
        (placed, placed, jax.ShapeDtypeStruct((2, turns * STEP + 2), I32)),
        [SMEM, SMEM, SMEM, VMEM, VMEM],
        (VMEM, VMEM, SMEM),
        [pltpu.SMEM((turns * STEP,), I32)],
        10,
        10**7,
        7 * 10**6,
        jnp.stack([core, here]).astype(I32),
        numbers,
        other_numbers,
        tiles,
        other_tiles,
    )

    weights = jnp.concatenate(
        [
            neighbor_weight,
            root_weight,
            features.reshape(NN, quarter, side).swapaxes(0, 1).reshape(quarter, width),
        ],
        axis=0,
    )
    line, weights = lax.optimization_barrier((line, weights))
    all_weights = exchange(jnp.broadcast_to(weights[None], (NN, *weights.shape)), OVER_X)

    by_distance = {0: line}
    for hops in (1, -1, 2, -2):
        by_distance[-hops % NY] = pass_on(line, hops)
    for hops in (1, -1):
        by_distance[-3 * hops % NY] = pass_on(by_distance[-2 * hops % NY], hops)
    middle = NZ * NN // 2
    far_low = pass_on(by_distance[6][:middle], 2)
    far_high = pass_on(by_distance[2][middle:], -2)

    whole = jax.ShapeDtypeStruct((rows, width), F32)
    flops = 2 * slots * rows * quarter * width
    line_size = NZ * NN
    near_own, near_other = call(
        near_kernel,
        "near",
        (whole, whole),
        [SMEM, VMEM, VMEM] + [ANY] * len(NEAR),
        (VMEM, VMEM),
        [
            pltpu.VMEM((len(NEAR) * line_size, quarter, side), BF16),
            pltpu.SemaphoreType.DMA((len(NEAR),)),
        ],
        20,
        flops,
        8 * 10**6,
        meta,
        left_own,
        left_other,
        *[by_distance[d] for d in NEAR],
    )
    part_own, part_other = call(
        far_kernel,
        "far",
        (whole, jax.ShapeDtypeStruct((rows, width), BF16)),
        [SMEM, VMEM, VMEM, VMEM, VMEM] + [ANY] * (len(FAR) + 1),
        (VMEM, VMEM),
        [
            pltpu.VMEM((rows, width), F32),
            pltpu.VMEM((len(FAR) * line_size, quarter, side), BF16),
            pltpu.SemaphoreType.DMA((len(FAR) + 1,)),
        ],
        20,
        flops // 2,
        6 * 10**6,
        meta,
        left_own,
        left_other,
        near_own,
        near_other,
        by_distance[FAR[0]],
        by_distance[FAR[1]],
        far_low,
        far_high,
    )
    copies = call(
        join_kernel,
        "join",
        jax.ShapeDtypeStruct((NN, rows, width), BF16),
        [VMEM, VMEM],
        VMEM,
        [],
        8,
        10**6,
        2 * 10**6,
        part_own,
        swap_cores(part_other),
    )
    parts = exchange(copies, OVER_X)

    layer_output, grads = call(
        dense_kernel,
        "dense",
        (
            jax.ShapeDtypeStruct((rows, side), BF16),
            jax.ShapeDtypeStruct((3 * NN, side, side), BF16),
        ),
        [SMEM] + [VMEM] * 5,
        (VMEM, VMEM),
        [pltpu.VMEM((rows, width), BF16)],
        16,
        12 * rows * width * width,
        5 * 10**6,
        narrow[None],
        parts,
        all_weights,
        features,
        cotangent,
        output_weight,
    )

    chunk = 3 * NN * side // (NZ * NC)

    def total(pieces, count):
        return call(
            total_kernel,
            "total",
            jax.ShapeDtypeStruct((count, chunk, side), BF16),
            [VMEM],
            VMEM,
            [],
            4,
            10**6,
            10**6,
            pieces,
        )

    summed = total(exchange(grads.reshape(NZ * NC, chunk, side), OVER_ZC), NY)
    summed = total(exchange(summed, OVER_Y), NZ * NC)
    full = exchange(summed, OVER_ZC).reshape(3 * NN, side, side)
    return layer_output, *call(
        last_kernel,
        "last",
        (
            jax.ShapeDtypeStruct((side, width), F32),
            jax.ShapeDtypeStruct((side, width), F32),
            jax.ShapeDtypeStruct((width, side), F32),
        ),
        [VMEM],
        (VMEM, VMEM, VMEM),
        [],
        4,
        10**6,
        10**6,
        full,
    )


def solution(mesh):
    return jax.shard_map(
        per_device,
        mesh=mesh,
        in_specs=(
            P("wide", "narrow"),
            P("wide", "narrow", None, None, None),
            P("wide", "narrow", None),
            P("wide", "narrow", None),
            P("wide", "narrow"),
            P("narrow", None),
            P("narrow", None),
            P(),
            P("wide", None),
        ),
        out_specs=(P("wide", "narrow"), P("narrow", None), P("narrow", None), P(None, "narrow")),
        check_vma=False,
    )
```

```python
import jax
import jax.numpy as jnp
from jax import lax
from jax.experimental import pallas as pl
from jax.experimental.pallas import tpu as pltpu
from jax.sharding import PartitionSpec as P

AXES = ("wide", "narrow")
NZ, NY, NC, NN = 8, 8, 2, 4
STEP = 8
VMEM = pl.BlockSpec(memory_space=pltpu.VMEM)
SMEM = pl.BlockSpec(memory_space=pltpu.SMEM)
ANY = pl.BlockSpec(memory_space=pl.ANY)
F32, BF16, I32 = jnp.float32, jnp.bfloat16, jnp.int32
NEAR = (0, 7, 1, 6, 2)
FAR = (5, 3, 4)
RING = [(FAR if d in FAR else NEAR).index(d) * NZ * NN for d in range(NY)] + [int(d in FAR) for d in range(NY)]


def places():
    for z in range(NZ):
        for y in range(NY):
            for c in range(NC):
                for n in range(NN):
                    yield z, y, c, n


def device(z, y, c, n):
    return ((z * NY + y) * NC + c) * NN + n


def groups(key):
    found = {}
    for place in places():
        found.setdefault(key(*place), []).append(device(*place))
    return list(found.values())


FIRST = groups(lambda z, y, c, n: (0, y) if c == 0 else (1, z))
OVER_X = groups(lambda z, y, c, n: (z, y, c))
NEARBY = groups(lambda z, y, c, n: (z // 2, y // 2, n))
ALONG_Y = groups(lambda z, y, c, n: (z, y % 2, c, n))
ALONG_Z = groups(lambda z, y, c, n: (z % 2, y, c, n))
OTHER_CORE = [(device(z, y, c, n), device(z, y, 1 - c, n)) for z, y, c, n in places()]


def exchange(pieces, groups_):
    return lax.all_to_all(pieces, AXES, 0, 0, axis_index_groups=groups_, tiled=True)


def swap_cores(value):
    return lax.ppermute(value, AXES, OTHER_CORE)


def pass_on(value, hops):
    pairs = []
    for z, y, c, n in places():
        to = (z, (y + hops) % NY, c, n) if c == 0 else ((z + hops) % NZ, y, c, n)
        pairs.append((device(z, y, c, n), device(*to)))
    return lax.ppermute(value, AXES, pairs)


def call(kernel, name, out_shape, in_specs, out_specs, scratch, vmem, flops, size, *args):
    return pl.pallas_call(
        kernel,
        out_shape=out_shape,
        in_specs=in_specs,
        out_specs=out_specs,
        scratch_shapes=scratch,
        compiler_params=pltpu.CompilerParams(vmem_limit_bytes=vmem << 20),
        cost_estimate=pl.CostEstimate(flops=flops, bytes_accessed=size, transcendentals=0),
        name=name,
    )(*args)


def place_kernel(where_ref, own_n_ref, other_n_ref, own_ref, other_ref, lo_ref, lt_ref, meta_ref, order, tiles, sems):
    slots, half = own_ref.shape[0], own_ref.shape[2] // 2
    side = own_ref.shape[1]
    copies = [
        pltpu.make_async_copy(ref, tiles.at[k], sems.at[k]) for k, ref in enumerate((own_ref, other_ref))
    ]
    for copy in copies:
        copy.start()
    room = meta_ref.shape[1] - 2
    first = where_ref[0] == 0
    here = where_ref[1]
    low = lax.broadcasted_iota(I32, own_ref.shape[1:], 1) < half
    for block, (n_ref, l_ref) in enumerate(((own_n_ref, lo_ref), (other_n_ref, lt_ref))):
        count = n_ref[2 * slots]
        for k in range(room):
            order[k] = -1
            meta_ref[block, k] = 0

        def assign(s, carry, block=block, n_ref=n_ref):
            near, far = carry
            col = n_ref[slots + s]
            z, y = lax.shift_right_logical(col, 3), lax.bitwise_and(col, 7)
            ring = jnp.where(first, y, z)
            inner = jnp.where(first, z, y)
            away = lax.bitwise_and(ring - here + NY, NY - 1)
            is_far = where_ref[2 + NY + away]
            at = jnp.where(is_far == 1, room - 1 - far, near)
            order[at] = s
            meta_ref[block, at] = where_ref[2 + away] + inner * NN
            return near + 1 - is_far, far + is_far

        near, far = lax.fori_loop(0, count, assign, (jnp.int32(0), jnp.int32(0)))
        near_turns = lax.shift_right_logical(near + STEP - 1, 3)
        far_turns = lax.shift_right_logical(far + STEP - 1, 3)
        meta_ref[block, room] = near_turns
        meta_ref[block, room + 1] = room // STEP - far_turns

        def one_pair(p, carry, block=block, n_ref=n_ref, l_ref=l_ref):
            slot_a, slot_b = order[2 * p], order[2 * p + 1]
            at_a, at_b = jnp.maximum(slot_a, 0), jnp.maximum(slot_b, 0)
            a, b = tiles[block, at_a].astype(F32), tiles[block, at_b].astype(F32)
            moved = pltpu.roll(jnp.where(first, b, a), half, 1)
            both = jnp.where(low, jnp.where(first, a, moved), jnp.where(first, moved, b))
            row_a = jnp.where(slot_a >= 0, n_ref[at_a], -1)
            row_b = jnp.where(slot_b >= 0, n_ref[at_b], -1)
            rows = jnp.where(low, row_a, row_b)
            for r in range(2):
                l_ref[p, r * side:(r + 1) * side, :] = jnp.where(rows == r, both, 0.0).astype(BF16)
            return carry

        copies[block].wait()
        lax.fori_loop(0, near_turns * (STEP // 2), one_pair, 0)
        lax.fori_loop((room // STEP - far_turns) * (STEP // 2), room // 2, one_pair, 0)


def add_turns(meta_ref, block, first_turn, last_turn, l_ref, blocks, acc):
    def one_turn(i, carry):
        left = jnp.concatenate([l_ref[i * (STEP // 2) + k] for k in range(STEP // 2)], axis=1)
        spots = [meta_ref[block, i * STEP + k] for k in range(STEP)]
        right = jnp.concatenate(
            [jnp.concatenate([blocks[spot + n] for spot in spots], axis=0) for n in range(NN)],
            axis=1,
        )
        acc[...] += jnp.dot(left, right, preferred_element_type=F32)
        return carry

    lax.fori_loop(first_turn, last_turn, one_turn, 0)


def bring(refs, blocks, sems):
    copies, at = [], 0
    for k, ref in enumerate(refs):
        copies.append(
            pltpu.make_async_copy(ref, blocks.at[pl.ds(at, ref.shape[0])], sems.at[k])
        )
        at += ref.shape[0]
    for copy in copies:
        copy.start()
    return copies


def spread_kernel(f_ref, out_ref):
    quarter = out_ref.shape[1]
    for j in range(out_ref.shape[0]):
        out_ref[j] = f_ref[j % NN * quarter:(j % NN + 1) * quarter, :]


def pack_kernel(nw_ref, rw_ref, f_ref, w_ref):
    side = nw_ref.shape[0]
    quarter = f_ref.shape[0] // NN
    for j in range(NN):
        w_ref[j, :side, :] = nw_ref[...]
        w_ref[j, side:2 * side, :] = rw_ref[...]
        for q in range(NN):
            w_ref[j, 2 * side:, q * side:(q + 1) * side] = f_ref[q * quarter:(q + 1) * quarter, :]


def near_kernel(meta_ref, lo_ref, lt_ref, *refs):
    *given, po_ref, pt_ref, blocks, sems = refs
    room = meta_ref.shape[1] - 2
    copies = bring(given, blocks, sems)
    po_ref[...] = jnp.zeros_like(po_ref)
    pt_ref[...] = jnp.zeros_like(pt_ref)
    for copy in copies:
        copy.wait()
    add_turns(meta_ref, 1, 0, meta_ref[1, room], lt_ref, blocks, pt_ref)
    add_turns(meta_ref, 0, 0, meta_ref[0, room], lo_ref, blocks, po_ref)


def far_kernel(meta_ref, lo_ref, lt_ref, no_ref, nt_ref, *refs):
    *given, po_ref, pt_ref, acc, blocks, sems = refs
    room = meta_ref.shape[1] - 2
    copies = bring(given, blocks, sems)
    acc[...] = nt_ref[...]
    po_ref[...] = no_ref[...]
    for copy in copies:
        copy.wait()
    add_turns(meta_ref, 1, meta_ref[1, room + 1], room // STEP, lt_ref, blocks, acc)
    pt_ref[...] = acc[...].astype(BF16)
    add_turns(meta_ref, 0, meta_ref[0, room + 1], room // STEP, lo_ref, blocks, po_ref)


def join_kernel(own_ref, came_ref, out_ref):
    joined = (own_ref[...] + came_ref[...].astype(F32)).astype(BF16)
    for j in range(out_ref.shape[0]):
        out_ref[j] = joined


def total_kernel(in_ref, out_ref):
    summed = in_ref[0].astype(F32)
    for j in range(1, in_ref.shape[0]):
        summed = summed + in_ref[j].astype(F32)
    summed = summed.astype(BF16)
    for j in range(out_ref.shape[0]):
        out_ref[j] = summed


def last_kernel(in_ref, neighbor_ref, root_ref, output_ref):
    side = in_ref.shape[1]
    for j in range(NN):
        neighbor_ref[:, j * side:(j + 1) * side] = in_ref[j].astype(F32)
        root_ref[:, j * side:(j + 1) * side] = in_ref[NN + j].astype(F32)
        output_ref[j * side:(j + 1) * side, :] = in_ref[2 * NN + j].astype(F32)


def dense_kernel(n_ref, a_ref, w_ref, f_ref, cot_ref, ow_ref, out_ref, g_ref, agg_ref):
    side = f_ref.shape[1]
    quarter = w_ref.shape[1] - 2 * side
    mine = pl.ds(pl.multiple_of(n_ref[0] * side, side), side)
    root_weight = jnp.concatenate([w_ref[j, side:2 * side, :] for j in range(NN)], axis=0)
    neighbor_weight = jnp.concatenate([w_ref[j, :side, :] for j in range(NN)], axis=0)
    rows = jnp.concatenate(
        [
            jnp.concatenate(
                [w_ref[j, 2 * side:, q * side:(q + 1) * side] for j in range(NN)], axis=1
            )
            for q in range(NN)
        ],
        axis=0,
    )
    hidden_grad = lax.dot_general(
        cot_ref[...], ow_ref[...], (((1,), (1,)), ((), ())), preferred_element_type=F32
    )
    agg = a_ref[0].astype(F32)
    for j in range(1, NN):
        agg = agg + a_ref[j].astype(F32)
    agg = agg.astype(BF16)
    agg_ref[...] = agg
    pre = jnp.dot(agg, neighbor_weight, preferred_element_type=F32) + jnp.dot(
        rows, root_weight, preferred_element_type=F32
    )
    s = jax.nn.sigmoid(pre)
    hidden = (pre * s).astype(BF16)
    pre_grad = (hidden_grad * s * (1.0 + pre * (1.0 - s))).astype(BF16)
    over_rows = (((0,), (0,)), ((), ()))
    parts = (
        lax.dot_general(agg_ref[:, mine], pre_grad, over_rows, preferred_element_type=F32),
        lax.dot_general(f_ref[...], pre_grad, over_rows, preferred_element_type=F32),
    )
    for k, part in enumerate(parts):
        for j in range(NN):
            g_ref[k * NN + j] = part[:, j * side:(j + 1) * side].astype(BF16)
    part = lax.dot_general(hidden, cot_ref[:, mine], over_rows, preferred_element_type=F32)
    for j in range(NN):
        g_ref[2 * NN + j] = part[j * side:(j + 1) * side, :].astype(BF16)
    out_ref[...] = (
        f_ref[...].astype(F32) + jnp.dot(hidden, ow_ref[:, mine], preferred_element_type=F32)
    ).astype(BF16)


def per_device(
    features,
    tile_blocks,
    tile_rows,
    tile_cols,
    tile_count,
    neighbor_weight,
    root_weight,
    output_weight,
    cotangent,
):
    rows, side = features.shape
    width = NN * side
    quarter = rows // NN
    slots = tile_rows.shape[-1]
    wide = lax.axis_index("wide")
    narrow = lax.axis_index("narrow").astype(I32)
    core = wide % NC
    here = jnp.where(core == 0, (wide // NC) % NY, wide // (NC * NY))

    tiles = tile_blocks[0, 0]
    numbers = jnp.concatenate([tile_rows[0, 0], tile_cols[0, 0], tile_count[0]])
    other_tiles = swap_cores(tiles)
    other_numbers = swap_cores(numbers)

    pieces = call(
        spread_kernel,
        "spread",
        jax.ShapeDtypeStruct((NZ * NN, quarter, side), BF16),
        [VMEM],
        VMEM,
        [],
        4,
        10**5,
        10**6,
        features,
    )
    line = exchange(pieces, FIRST)

    turns = (slots + 2 * STEP - 2) // STEP
    placed = jax.ShapeDtypeStruct((turns * STEP // 2, rows, side), BF16)
    left_own, left_other, meta = call(
        place_kernel,
        "place",
        (placed, placed, jax.ShapeDtypeStruct((2, turns * STEP + 2), I32)),
        [SMEM, SMEM, SMEM, ANY, ANY],
        (VMEM, VMEM, SMEM),
        [
            pltpu.SMEM((turns * STEP,), I32),
            pltpu.VMEM((2, *tiles.shape), BF16),
            pltpu.SemaphoreType.DMA((2,)),
        ],
        10,
        10**7,
        7 * 10**6,
        jnp.concatenate([jnp.stack([core, here]).astype(I32), jnp.array(RING, I32)]),
        numbers,
        other_numbers,
        tiles,
        other_tiles,
    )

    weights = call(
        pack_kernel,
        "pack",
        jax.ShapeDtypeStruct((NN, 2 * side + quarter, width), BF16),
        [VMEM, VMEM, VMEM],
        VMEM,
        [],
        4,
        10**5,
        2 * 10**6,
        neighbor_weight,
        root_weight,
        features,
    )
    line, meta, weights = lax.optimization_barrier((line, meta, weights))
    all_weights = exchange(weights, OVER_X)
    by_distance = {0: line}
    for hops in (1, -1, 2, -2):
        by_distance[-hops % NY] = pass_on(line, hops)
    arrived = lax.optimization_barrier([by_distance[d] for d in NEAR[1:]])
    by_distance.update(zip(NEAR[1:], arrived))
    by_distance[4] = pass_on(by_distance[6], 2)
    for hops in (1, -1):
        by_distance[-3 * hops % NY] = pass_on(by_distance[-2 * hops % NY], hops)
    whole = jax.ShapeDtypeStruct((rows, width), F32)
    flops = 2 * slots * rows * quarter * width
    line_size = NZ * NN
    near_own, near_other = call(
        near_kernel,
        "near",
        (whole, whole),
        [SMEM, VMEM, VMEM] + [ANY] * len(NEAR),
        (VMEM, VMEM),
        [
            pltpu.VMEM((len(NEAR) * line_size, quarter, side), BF16),
            pltpu.SemaphoreType.DMA((len(NEAR),)),
        ],
        20,
        flops,
        8 * 10**6,
        meta,
        left_own,
        left_other,
        *[by_distance[d] for d in NEAR],
    )
    part_own, part_other = call(
        far_kernel,
        "far",
        (whole, jax.ShapeDtypeStruct((rows, width), BF16)),
        [SMEM, VMEM, VMEM, VMEM, VMEM] + [ANY] * len(FAR),
        (VMEM, VMEM),
        [
            pltpu.VMEM((rows, width), F32),
            pltpu.VMEM((len(FAR) * line_size, quarter, side), BF16),
            pltpu.SemaphoreType.DMA((len(FAR),)),
        ],
        20,
        flops // 2,
        6 * 10**6,
        meta,
        left_own,
        left_other,
        near_own,
        near_other,
        *[by_distance[d] for d in FAR],
    )
    copies = call(
        join_kernel,
        "join",
        jax.ShapeDtypeStruct((NN, rows, width), BF16),
        [VMEM, VMEM],
        VMEM,
        [],
        8,
        10**6,
        2 * 10**6,
        part_own,
        swap_cores(part_other),
    )
    parts = exchange(copies, OVER_X)

    layer_output, grads = call(
        dense_kernel,
        "dense",
        (
            jax.ShapeDtypeStruct((rows, side), BF16),
            jax.ShapeDtypeStruct((3 * NN, side, side), BF16),
        ),
        [SMEM] + [VMEM] * 5,
        (VMEM, VMEM),
        [pltpu.VMEM((rows, width), BF16)],
        16,
        12 * rows * width * width,
        5 * 10**6,
        narrow[None],
        parts,
        all_weights,
        features,
        cotangent,
        output_weight,
    )

    nearby = len(NEARBY[0])
    chunk = 3 * NN * side // nearby

    def total(pieces, count):
        return call(
            total_kernel,
            "total",
            jax.ShapeDtypeStruct((count, chunk, side), BF16),
            [VMEM],
            VMEM,
            [],
            4,
            10**6,
            10**6,
            pieces,
        )

    summed = total(exchange(grads.reshape(nearby, chunk, side), NEARBY), NY // 2)
    summed = total(exchange(summed, ALONG_Y), NZ // 2)
    summed = total(exchange(summed, ALONG_Z), nearby)
    full = exchange(summed, NEARBY).reshape(3 * NN, side, side)
    return layer_output, *call(
        last_kernel,
        "last",
        (
            jax.ShapeDtypeStruct((side, width), F32),
            jax.ShapeDtypeStruct((side, width), F32),
            jax.ShapeDtypeStruct((width, side), F32),
        ),
        [VMEM],
        (VMEM, VMEM, VMEM),
        [],
        4,
        10**6,
        10**6,
        full,
    )


def solution(mesh):
    return jax.shard_map(
        per_device,
        mesh=mesh,
        in_specs=(
            P("wide", "narrow"),
            P("wide", "narrow", None, None, None),
            P("wide", "narrow", None),
            P("wide", "narrow", None),
            P("wide", "narrow"),
            P("narrow", None),
            P("narrow", None),
            P(),
            P("wide", None),
        ),
        out_specs=(P("wide", "narrow"), P("narrow", None), P("narrow", None), P(None, "narrow")),
        check_vma=False,
    )
```

```python
import jax
import jax.numpy as jnp
from jax import lax
from jax.experimental import pallas as pl
from jax.experimental.pallas import tpu as pltpu
from jax.sharding import PartitionSpec as P

AXES = ("wide", "narrow")
NZ, NY, NC, NN = 8, 8, 2, 4
STEP = 8
VMEM = pl.BlockSpec(memory_space=pltpu.VMEM)
SMEM = pl.BlockSpec(memory_space=pltpu.SMEM)
ANY = pl.BlockSpec(memory_space=pl.ANY)
F32, BF16, I32 = jnp.float32, jnp.bfloat16, jnp.int32
NEAR = (0, 6, 2, 7, 1)
FAR = (4, 5, 3)
RING = [(FAR if d in FAR else NEAR).index(d) * NZ * NN for d in range(NY)] + [int(d in FAR) for d in range(NY)]


def places():
    for z in range(NZ):
        for y in range(NY):
            for c in range(NC):
                for n in range(NN):
                    yield z, y, c, n


def device(z, y, c, n):
    return ((z * NY + y) * NC + c) * NN + n


def groups(key):
    found = {}
    for place in places():
        found.setdefault(key(*place), []).append(device(*place))
    return list(found.values())


FIRST = groups(lambda z, y, c, n: (0, y) if c == 0 else (1, z))
OVER_X = groups(lambda z, y, c, n: (z, y, c))
NEARBY = groups(lambda z, y, c, n: (z // 2, y // 2, n))
ALONG_Y = groups(lambda z, y, c, n: (z, y % 2, c, n))
ALONG_Z = groups(lambda z, y, c, n: (z % 2, y, c, n))
OTHER_CORE = [(device(z, y, c, n), device(z, y, 1 - c, n)) for z, y, c, n in places()]


def exchange(pieces, groups_):
    return lax.all_to_all(pieces, AXES, 0, 0, axis_index_groups=groups_, tiled=True)


def swap_cores(value):
    return lax.ppermute(value, AXES, OTHER_CORE)


def pass_on(value, hops):
    pairs = []
    for z, y, c, n in places():
        to = (z, (y + hops) % NY, c, n) if c == 0 else ((z + hops) % NZ, y, c, n)
        pairs.append((device(z, y, c, n), device(*to)))
    return lax.ppermute(value, AXES, pairs)


def call(kernel, name, out_shape, in_specs, out_specs, scratch, vmem, flops, size, *args):
    return pl.pallas_call(
        kernel,
        out_shape=out_shape,
        in_specs=in_specs,
        out_specs=out_specs,
        scratch_shapes=scratch,
        compiler_params=pltpu.CompilerParams(vmem_limit_bytes=vmem << 20),
        cost_estimate=pl.CostEstimate(flops=flops, bytes_accessed=size, transcendentals=0),
        name=name,
    )(*args)


def place_kernel(where_ref, own_n_ref, other_n_ref, own_ref, other_ref, lo_ref, lt_ref, meta_ref, order, tiles, sems):
    slots, half = own_ref.shape[0], own_ref.shape[2] // 2
    side = own_ref.shape[1]
    copies = [
        pltpu.make_async_copy(ref, tiles.at[k], sems.at[k]) for k, ref in enumerate((own_ref, other_ref))
    ]
    for copy in copies:
        copy.start()
    room = meta_ref.shape[1] - 2
    first = where_ref[0] == 0
    here = where_ref[1]
    low = lax.broadcasted_iota(I32, own_ref.shape[1:], 1) < half
    for block, (n_ref, l_ref) in enumerate(((own_n_ref, lo_ref), (other_n_ref, lt_ref))):
        count = n_ref[2 * slots]
        for k in range(room):
            order[k] = -1
            meta_ref[block, k] = 0

        def assign(s, carry, block=block, n_ref=n_ref):
            near, far = carry
            col = n_ref[slots + s]
            z, y = lax.shift_right_logical(col, 3), lax.bitwise_and(col, 7)
            ring = jnp.where(first, y, z)
            inner = jnp.where(first, z, y)
            away = lax.bitwise_and(ring - here + NY, NY - 1)
            is_far = where_ref[2 + NY + away]
            at = jnp.where(is_far == 1, room - 1 - far, near)
            order[at] = s
            meta_ref[block, at] = where_ref[2 + away] + inner * NN
            return near + 1 - is_far, far + is_far

        near, far = lax.fori_loop(0, count, assign, (jnp.int32(0), jnp.int32(0)))
        near_turns = lax.shift_right_logical(near + STEP - 1, 3)
        far_turns = lax.shift_right_logical(far + STEP - 1, 3)
        meta_ref[block, room] = near_turns
        meta_ref[block, room + 1] = room // STEP - far_turns

        def one_pair(p, carry, block=block, n_ref=n_ref, l_ref=l_ref):
            slot_a, slot_b = order[2 * p], order[2 * p + 1]
            at_a, at_b = jnp.maximum(slot_a, 0), jnp.maximum(slot_b, 0)
            a, b = tiles[block, at_a].astype(F32), tiles[block, at_b].astype(F32)
            moved = pltpu.roll(jnp.where(first, b, a), half, 1)
            both = jnp.where(low, jnp.where(first, a, moved), jnp.where(first, moved, b))
            row_a = jnp.where(slot_a >= 0, n_ref[at_a], -1)
            row_b = jnp.where(slot_b >= 0, n_ref[at_b], -1)
            rows = jnp.where(low, row_a, row_b)
            for r in range(2):
                l_ref[p, r * side:(r + 1) * side, :] = jnp.where(rows == r, both, 0.0).astype(BF16)
            return carry

        copies[block].wait()
        lax.fori_loop(0, near_turns * (STEP // 2), one_pair, 0)
        lax.fori_loop((room // STEP - far_turns) * (STEP // 2), room // 2, one_pair, 0)


def add_turns(meta_ref, block, first_turn, last_turn, l_ref, blocks, acc):
    def one_turn(i, carry):
        left = jnp.concatenate([l_ref[i * (STEP // 2) + k] for k in range(STEP // 2)], axis=1)
        spots = [meta_ref[block, i * STEP + k] for k in range(STEP)]
        right = jnp.concatenate(
            [jnp.concatenate([blocks[spot + n] for spot in spots], axis=0) for n in range(NN)],
            axis=1,
        )
        acc[...] += jnp.dot(left, right, preferred_element_type=F32)
        return carry

    lax.fori_loop(first_turn, last_turn, one_turn, 0)


def bring(refs, blocks, sems):
    copies, at = [], 0
    for k, ref in enumerate(refs):
        copies.append(
            pltpu.make_async_copy(ref, blocks.at[pl.ds(at, ref.shape[0])], sems.at[k])
        )
        at += ref.shape[0]
    for copy in copies:
        copy.start()
    return copies


def spread_kernel(f_ref, out_ref):
    quarter = out_ref.shape[1]
    for j in range(out_ref.shape[0]):
        out_ref[j] = f_ref[j % NN * quarter:(j % NN + 1) * quarter, :]


def pack_kernel(nw_ref, rw_ref, f_ref, w_ref):
    side = nw_ref.shape[0]
    quarter = f_ref.shape[0] // NN
    for j in range(NN):
        w_ref[j, :side, :] = nw_ref[...]
        w_ref[j, side:2 * side, :] = rw_ref[...]
        for q in range(NN):
            w_ref[j, 2 * side:, q * side:(q + 1) * side] = f_ref[q * quarter:(q + 1) * quarter, :]


def near_kernel(meta_ref, lo_ref, lt_ref, *refs):
    *given, po_ref, pt_ref, blocks, sems = refs
    room = meta_ref.shape[1] - 2
    copies = bring(given, blocks, sems)
    po_ref[...] = jnp.zeros_like(po_ref)
    pt_ref[...] = jnp.zeros_like(pt_ref)
    for copy in copies:
        copy.wait()
    add_turns(meta_ref, 1, 0, meta_ref[1, room], lt_ref, blocks, pt_ref)
    add_turns(meta_ref, 0, 0, meta_ref[0, room], lo_ref, blocks, po_ref)


def far_kernel(meta_ref, lo_ref, lt_ref, no_ref, nt_ref, *refs):
    *given, po_ref, pt_ref, acc, blocks, sems = refs
    room = meta_ref.shape[1] - 2
    copies = bring(given, blocks, sems)
    acc[...] = nt_ref[...]
    po_ref[...] = no_ref[...]
    for copy in copies:
        copy.wait()
    add_turns(meta_ref, 1, meta_ref[1, room + 1], room // STEP, lt_ref, blocks, acc)
    pt_ref[...] = acc[...].astype(BF16)
    add_turns(meta_ref, 0, meta_ref[0, room + 1], room // STEP, lo_ref, blocks, po_ref)


def join_kernel(own_ref, came_ref, *out_refs):
    joined = (own_ref[...] + came_ref[...].astype(F32)).astype(BF16)
    part = joined.shape[1] // len(out_refs)
    for k, out_ref in enumerate(out_refs):
        for j in range(out_ref.shape[0]):
            out_ref[j] = joined[:, k * part:(k + 1) * part]


def total_kernel(in_ref, out_ref):
    summed = in_ref[0].astype(F32)
    for j in range(1, in_ref.shape[0]):
        summed = summed + in_ref[j].astype(F32)
    summed = summed.astype(BF16)
    for j in range(out_ref.shape[0]):
        out_ref[j] = summed


def last_kernel(in_ref, neighbor_ref, root_ref, output_ref):
    side = in_ref.shape[1]
    for j in range(NN):
        neighbor_ref[:, j * side:(j + 1) * side] = in_ref[j].astype(F32)
        root_ref[:, j * side:(j + 1) * side] = in_ref[NN + j].astype(F32)
        output_ref[j * side:(j + 1) * side, :] = in_ref[2 * NN + j].astype(F32)


def dense_kernel(n_ref, a_ref, b_ref, w_ref, f_ref, cot_ref, ow_ref, out_ref, g_ref, agg_ref):
    side = f_ref.shape[1]
    quarter = w_ref.shape[1] - 2 * side
    mine = pl.ds(pl.multiple_of(n_ref[0] * side, side), side)
    root_weight = jnp.concatenate([w_ref[j, side:2 * side, :] for j in range(NN)], axis=0)
    neighbor_weight = jnp.concatenate([w_ref[j, :side, :] for j in range(NN)], axis=0)
    rows = jnp.concatenate(
        [
            jnp.concatenate(
                [w_ref[j, 2 * side:, q * side:(q + 1) * side] for j in range(NN)], axis=1
            )
            for q in range(NN)
        ],
        axis=0,
    )
    hidden_grad = lax.dot_general(
        cot_ref[...], ow_ref[...], (((1,), (1,)), ((), ())), preferred_element_type=F32
    )
    halves = []
    for half_ref in (a_ref, b_ref):
        half = half_ref[0].astype(F32)
        for j in range(1, NN):
            half = half + half_ref[j].astype(F32)
        halves.append(half.astype(BF16))
    agg = jnp.concatenate(halves, axis=1)
    agg_ref[...] = agg
    pre = jnp.dot(agg, neighbor_weight, preferred_element_type=F32) + jnp.dot(
        rows, root_weight, preferred_element_type=F32
    )
    s = jax.nn.sigmoid(pre)
    hidden = (pre * s).astype(BF16)
    pre_grad = (hidden_grad * s * (1.0 + pre * (1.0 - s))).astype(BF16)
    over_rows = (((0,), (0,)), ((), ()))
    parts = (
        lax.dot_general(agg_ref[:, mine], pre_grad, over_rows, preferred_element_type=F32),
        lax.dot_general(f_ref[...], pre_grad, over_rows, preferred_element_type=F32),
    )
    for k, part in enumerate(parts):
        for j in range(NN):
            g_ref[k * NN + j] = part[:, j * side:(j + 1) * side].astype(BF16)
    part = lax.dot_general(hidden, cot_ref[:, mine], over_rows, preferred_element_type=F32)
    for j in range(NN):
        g_ref[2 * NN + j] = part[j * side:(j + 1) * side, :].astype(BF16)
    out_ref[...] = (
        f_ref[...].astype(F32) + jnp.dot(hidden, ow_ref[:, mine], preferred_element_type=F32)
    ).astype(BF16)


def per_device(
    features,
    tile_blocks,
    tile_rows,
    tile_cols,
    tile_count,
    neighbor_weight,
    root_weight,
    output_weight,
    cotangent,
):
    rows, side = features.shape
    width = NN * side
    quarter = rows // NN
    slots = tile_rows.shape[-1]
    wide = lax.axis_index("wide")
    narrow = lax.axis_index("narrow").astype(I32)
    core = wide % NC
    here = jnp.where(core == 0, (wide // NC) % NY, wide // (NC * NY))

    tiles = tile_blocks[0, 0]
    numbers = jnp.concatenate([tile_rows[0, 0], tile_cols[0, 0], tile_count[0]])
    other_tiles = swap_cores(tiles)
    other_numbers = swap_cores(numbers)

    pieces = call(
        spread_kernel,
        "spread",
        jax.ShapeDtypeStruct((NZ * NN, quarter, side), BF16),
        [VMEM],
        VMEM,
        [],
        4,
        10**5,
        10**6,
        features,
    )
    line = exchange(pieces, FIRST)

    weights = call(
        pack_kernel,
        "pack",
        jax.ShapeDtypeStruct((NN, 2 * side + quarter, width), BF16),
        [VMEM, VMEM, VMEM],
        VMEM,
        [],
        4,
        10**5,
        2 * 10**6,
        neighbor_weight,
        root_weight,
        features,
    )
    line, weights, other_numbers = lax.optimization_barrier((line, weights, other_numbers))
    all_weights = exchange(weights, OVER_X)
    by_distance = {0: line}
    for hops in (2, -2, 1, -1):
        by_distance[-hops % NY] = pass_on(line, hops)
    arrived = lax.optimization_barrier([by_distance[d] for d in NEAR[1:]])
    by_distance.update(zip(NEAR[1:], arrived))
    for hops in (1, -1):
        by_distance[-3 * hops % NY] = pass_on(by_distance[-2 * hops % NY], hops)
    by_distance[4] = pass_on(by_distance[6], 2)
    turns = (slots + 2 * STEP - 2) // STEP
    placed = jax.ShapeDtypeStruct((turns * STEP // 2, rows, side), BF16)
    left_own, left_other, meta = call(
        place_kernel,
        "place",
        (placed, placed, jax.ShapeDtypeStruct((2, turns * STEP + 2), I32)),
        [SMEM, SMEM, SMEM, ANY, ANY],
        (VMEM, VMEM, SMEM),
        [
            pltpu.SMEM((turns * STEP,), I32),
            pltpu.VMEM((2, *tiles.shape), BF16),
            pltpu.SemaphoreType.DMA((2,)),
        ],
        10,
        10**7,
        7 * 10**6,
        jnp.concatenate([jnp.stack([core, here]).astype(I32), jnp.array(RING, I32)]),
        numbers,
        other_numbers,
        tiles,
        other_tiles,
    )

    whole = jax.ShapeDtypeStruct((rows, width), F32)
    flops = 2 * slots * rows * quarter * width
    line_size = NZ * NN
    near_own, near_other = call(
        near_kernel,
        "near",
        (whole, whole),
        [SMEM, VMEM, VMEM] + [ANY] * len(NEAR),
        (VMEM, VMEM),
        [
            pltpu.VMEM((len(NEAR) * line_size, quarter, side), BF16),
            pltpu.SemaphoreType.DMA((len(NEAR),)),
        ],
        20,
        flops,
        8 * 10**6,
        meta,
        left_own,
        left_other,
        *[by_distance[d] for d in NEAR],
    )
    part_own, part_other = call(
        far_kernel,
        "far",
        (whole, jax.ShapeDtypeStruct((rows, width), BF16)),
        [SMEM, VMEM, VMEM, VMEM, VMEM] + [ANY] * len(FAR),
        (VMEM, VMEM),
        [
            pltpu.VMEM((rows, width), F32),
            pltpu.VMEM((len(FAR) * line_size, quarter, side), BF16),
            pltpu.SemaphoreType.DMA((len(FAR),)),
        ],
        20,
        flops // 2,
        6 * 10**6,
        meta,
        left_own,
        left_other,
        near_own,
        near_other,
        *[by_distance[d] for d in FAR],
    )
    copies = call(
        join_kernel,
        "join",
        (jax.ShapeDtypeStruct((NN, rows, width // 2), BF16),) * 2,
        [VMEM, VMEM],
        (VMEM, VMEM),
        [],
        8,
        10**6,
        2 * 10**6,
        part_own,
        swap_cores(part_other),
    )
    parts = [exchange(copy, OVER_X) for copy in copies]

    layer_output, grads = call(
        dense_kernel,
        "dense",
        (
            jax.ShapeDtypeStruct((rows, side), BF16),
            jax.ShapeDtypeStruct((3 * NN, side, side), BF16),
        ),
        [SMEM] + [VMEM] * 6,
        (VMEM, VMEM),
        [pltpu.VMEM((rows, width), BF16)],
        16,
        12 * rows * width * width,
        5 * 10**6,
        narrow[None],
        *parts,
        all_weights,
        features,
        cotangent,
        output_weight,
    )

    nearby = len(NEARBY[0])
    chunk = 3 * NN * side // nearby

    def total(pieces, count):
        return call(
            total_kernel,
            "total",
            jax.ShapeDtypeStruct((count, chunk, side), BF16),
            [VMEM],
            VMEM,
            [],
            4,
            10**6,
            10**6,
            pieces,
        )

    summed = total(exchange(grads.reshape(nearby, chunk, side), NEARBY), NY // 2)
    summed = total(exchange(summed, ALONG_Y), NZ // 2)
    summed = total(exchange(summed, ALONG_Z), nearby)
    full = exchange(summed, NEARBY).reshape(3 * NN, side, side)
    return layer_output, *call(
        last_kernel,
        "last",
        (
            jax.ShapeDtypeStruct((side, width), F32),
            jax.ShapeDtypeStruct((side, width), F32),
            jax.ShapeDtypeStruct((width, side), F32),
        ),
        [VMEM],
        (VMEM, VMEM, VMEM),
        [],
        4,
        10**6,
        10**6,
        full,
    )


def solution(mesh):
    return jax.shard_map(
        per_device,
        mesh=mesh,
        in_specs=(
            P("wide", "narrow"),
            P("wide", "narrow", None, None, None),
            P("wide", "narrow", None),
            P("wide", "narrow", None),
            P("wide", "narrow"),
            P("narrow", None),
            P("narrow", None),
            P(),
            P("wide", None),
        ),
        out_specs=(P("wide", "narrow"), P("narrow", None), P("narrow", None), P(None, "narrow")),
        check_vma=False,
    )
```

```python
import jax
import jax.numpy as jnp
from jax import lax
from jax.experimental import pallas as pl
from jax.experimental.pallas import tpu as pltpu
from jax.sharding import PartitionSpec as P

AXES = ("wide", "narrow")
NZ, NY, NC, NN = 8, 8, 2, 4
STEP = 8
VMEM = pl.BlockSpec(memory_space=pltpu.VMEM)
SMEM = pl.BlockSpec(memory_space=pltpu.SMEM)
ANY = pl.BlockSpec(memory_space=pl.ANY)
HBM = pl.BlockSpec(memory_space=pltpu.HBM)
F32, BF16, I32 = jnp.float32, jnp.bfloat16, jnp.int32
NEAR = (0, 6, 2, 7, 1)
FAR = (4, 5, 3)
RING = [(FAR if d in FAR else NEAR).index(d) * NZ * NN for d in range(NY)] + [int(d in FAR) for d in range(NY)]


def places():
    for z in range(NZ):
        for y in range(NY):
            for c in range(NC):
                for n in range(NN):
                    yield z, y, c, n


def device(z, y, c, n):
    return ((z * NY + y) * NC + c) * NN + n


def groups(key):
    found = {}
    for place in places():
        found.setdefault(key(*place), []).append(device(*place))
    return list(found.values())


FIRST = groups(lambda z, y, c, n: (0, y) if c == 0 else (1, z))
OVER_X = groups(lambda z, y, c, n: (z, y, c))
NEARBY = groups(lambda z, y, c, n: (z // 2, y // 2, n))
ALONG_Y = groups(lambda z, y, c, n: (z, y % 2, c, n))
ALONG_Z = groups(lambda z, y, c, n: (z % 2, y, c, n))
OTHER_CORE = [(device(z, y, c, n), device(z, y, 1 - c, n)) for z, y, c, n in places()]


def exchange(pieces, groups_):
    return lax.all_to_all(pieces, AXES, 0, 0, axis_index_groups=groups_, tiled=True)


def swap_cores(value):
    return lax.ppermute(value, AXES, OTHER_CORE)


def pass_on(value, hops):
    pairs = []
    for z, y, c, n in places():
        to = (z, (y + hops) % NY, c, n) if c == 0 else ((z + hops) % NZ, y, c, n)
        pairs.append((device(z, y, c, n), device(*to)))
    return lax.ppermute(value, AXES, pairs)


def call(kernel, name, out_shape, in_specs, out_specs, scratch, vmem, flops, size, *args):
    return pl.pallas_call(
        kernel,
        out_shape=out_shape,
        in_specs=in_specs,
        out_specs=out_specs,
        scratch_shapes=scratch,
        compiler_params=pltpu.CompilerParams(vmem_limit_bytes=vmem << 20),
        cost_estimate=pl.CostEstimate(flops=flops, bytes_accessed=size, transcendentals=0),
        name=name,
    )(*args)


def place_kernel(where_ref, own_n_ref, other_n_ref, own_ref, other_ref, lo_ref, lt_ref, meta_ref, order, tiles, sems):
    slots, half = own_ref.shape[0], own_ref.shape[2] // 2
    side = own_ref.shape[1]
    copies = [
        pltpu.make_async_copy(ref, tiles.at[k], sems.at[k]) for k, ref in enumerate((own_ref, other_ref))
    ]
    for copy in copies:
        copy.start()
    room = meta_ref.shape[1] - 2
    first = where_ref[0] == 0
    here = where_ref[1]
    low = lax.broadcasted_iota(I32, own_ref.shape[1:], 1) < half
    for block, (n_ref, l_ref) in enumerate(((own_n_ref, lo_ref), (other_n_ref, lt_ref))):
        count = n_ref[2 * slots]
        for k in range(room):
            order[k] = -1
            meta_ref[block, k] = 0

        def assign(s, carry, block=block, n_ref=n_ref):
            near, far = carry
            col = n_ref[slots + s]
            z, y = lax.shift_right_logical(col, 3), lax.bitwise_and(col, 7)
            ring = jnp.where(first, y, z)
            inner = jnp.where(first, z, y)
            away = lax.bitwise_and(ring - here + NY, NY - 1)
            is_far = where_ref[2 + NY + away]
            at = jnp.where(is_far == 1, room - 1 - far, near)
            order[at] = s
            meta_ref[block, at] = where_ref[2 + away] + inner * NN
            return near + 1 - is_far, far + is_far

        near, far = lax.fori_loop(0, count, assign, (jnp.int32(0), jnp.int32(0)))
        near_turns = lax.shift_right_logical(near + STEP - 1, 3)
        far_turns = lax.shift_right_logical(far + STEP - 1, 3)
        meta_ref[block, room] = near_turns
        meta_ref[block, room + 1] = room // STEP - far_turns

        def one_pair(p, carry, block=block, n_ref=n_ref, l_ref=l_ref):
            slot_a, slot_b = order[2 * p], order[2 * p + 1]
            at_a, at_b = jnp.maximum(slot_a, 0), jnp.maximum(slot_b, 0)
            a, b = tiles[block, at_a].astype(F32), tiles[block, at_b].astype(F32)
            moved = pltpu.roll(jnp.where(first, b, a), half, 1)
            both = jnp.where(low, jnp.where(first, a, moved), jnp.where(first, moved, b))
            row_a = jnp.where(slot_a >= 0, n_ref[at_a], -1)
            row_b = jnp.where(slot_b >= 0, n_ref[at_b], -1)
            rows = jnp.where(low, row_a, row_b)
            for r in range(2):
                l_ref[p, r * side:(r + 1) * side, :] = jnp.where(rows == r, both, 0.0).astype(BF16)
            return carry

        copies[block].wait()
        lax.fori_loop(0, near_turns * (STEP // 2), one_pair, 0)
        lax.fori_loop((room // STEP - far_turns) * (STEP // 2), room // 2, one_pair, 0)


def add_turns(meta_ref, block, first_turn, last_turn, l_ref, blocks, acc):
    def one_turn(i, carry):
        left = jnp.concatenate([l_ref[i * (STEP // 2) + k] for k in range(STEP // 2)], axis=1)
        spots = [meta_ref[block, i * STEP + k] for k in range(STEP)]
        right = jnp.concatenate(
            [jnp.concatenate([blocks[spot + n] for spot in spots], axis=0) for n in range(NN)],
            axis=1,
        )
        acc[...] += jnp.dot(left, right, preferred_element_type=F32)
        return carry

    lax.fori_loop(first_turn, last_turn, one_turn, 0)


def bring(refs, blocks, sems):
    copies, at = [], 0
    for k, ref in enumerate(refs):
        copies.append(
            pltpu.make_async_copy(ref, blocks.at[pl.ds(at, ref.shape[0])], sems.at[k])
        )
        at += ref.shape[0]
    for copy in copies:
        copy.start()
    return copies


def fetch(sources, targets, sems):
    copies = [
        pltpu.make_async_copy(source, target, sems.at[k])
        for k, (source, target) in enumerate(zip(sources, targets))
    ]
    for copy in copies:
        copy.start()
    return copies


def spread_kernel(f_from, out_ref, f_ref, sems):
    for copy in fetch((f_from,), (f_ref,), sems):
        copy.wait()
    quarter = out_ref.shape[1]
    for j in range(out_ref.shape[0]):
        out_ref[j] = f_ref[j % NN * quarter:(j % NN + 1) * quarter, :]


def pack_kernel(nw_from, rw_from, f_from, w_ref, nw_ref, rw_ref, f_ref, sems):
    for copy in fetch((nw_from, rw_from, f_from), (nw_ref, rw_ref, f_ref), sems):
        copy.wait()
    side = nw_ref.shape[0]
    quarter = f_ref.shape[0] // NN
    for j in range(NN):
        w_ref[j, :side, :] = nw_ref[...]
        w_ref[j, side:2 * side, :] = rw_ref[...]
        for q in range(NN):
            w_ref[j, 2 * side:, q * side:(q + 1) * side] = f_ref[q * quarter:(q + 1) * quarter, :]


def near_kernel(meta_ref, lo_ref, lt_ref, *refs):
    *given, po_ref, pt_ref, blocks, sems = refs
    room = meta_ref.shape[1] - 2
    copies = bring(given, blocks, sems)
    po_ref[...] = jnp.zeros_like(po_ref)
    pt_ref[...] = jnp.zeros_like(pt_ref)
    for copy in copies:
        copy.wait()
    add_turns(meta_ref, 1, 0, meta_ref[1, room], lt_ref, blocks, pt_ref)
    add_turns(meta_ref, 0, 0, meta_ref[0, room], lo_ref, blocks, po_ref)


def far_kernel(meta_ref, lo_ref, lt_ref, no_ref, nt_ref, *refs):
    *given, po_ref, pt_ref, acc, blocks, sems = refs
    room = meta_ref.shape[1] - 2
    copies = bring(given, blocks, sems)
    acc[...] = nt_ref[...]
    po_ref[...] = no_ref[...]
    for copy in copies:
        copy.wait()
    add_turns(meta_ref, 1, meta_ref[1, room + 1], room // STEP, lt_ref, blocks, acc)
    pt_ref[...] = acc[...].astype(BF16)
    add_turns(meta_ref, 0, meta_ref[0, room + 1], room // STEP, lo_ref, blocks, po_ref)


def join_kernel(own_ref, came_ref, out_ref):
    joined = (own_ref[...] + came_ref[...].astype(F32)).astype(BF16)
    for j in range(out_ref.shape[0]):
        out_ref[j] = joined


def total_kernel(in_ref, out_ref):
    summed = in_ref[0].astype(F32)
    for j in range(1, in_ref.shape[0]):
        summed = summed + in_ref[j].astype(F32)
    summed = summed.astype(BF16)
    for j in range(out_ref.shape[0]):
        out_ref[j] = summed


def last_kernel(in_ref, neighbor_ref, root_ref, output_ref):
    side = in_ref.shape[1]
    for j in range(NN):
        neighbor_ref[:, j * side:(j + 1) * side] = in_ref[j].astype(F32)
        root_ref[:, j * side:(j + 1) * side] = in_ref[NN + j].astype(F32)
        output_ref[j * side:(j + 1) * side, :] = in_ref[2 * NN + j].astype(F32)


def dense_kernel(n_ref, a_ref, w_ref, f_ref, cot_ref, ow_ref, out_ref, g_ref, agg_ref):
    side = f_ref.shape[1]
    quarter = w_ref.shape[1] - 2 * side
    mine = pl.ds(pl.multiple_of(n_ref[0] * side, side), side)
    root_weight = jnp.concatenate([w_ref[j, side:2 * side, :] for j in range(NN)], axis=0)
    neighbor_weight = jnp.concatenate([w_ref[j, :side, :] for j in range(NN)], axis=0)
    rows = jnp.concatenate(
        [
            jnp.concatenate(
                [w_ref[j, 2 * side:, q * side:(q + 1) * side] for j in range(NN)], axis=1
            )
            for q in range(NN)
        ],
        axis=0,
    )
    agg = a_ref[0].astype(F32)
    for j in range(1, NN):
        agg = agg + a_ref[j].astype(F32)
    agg = agg.astype(BF16)
    agg_ref[...] = agg
    pre = jnp.dot(agg, neighbor_weight, preferred_element_type=F32) + jnp.dot(
        rows, root_weight, preferred_element_type=F32
    )
    hidden_grad = lax.dot_general(
        cot_ref[...], ow_ref[...], (((1,), (1,)), ((), ())), preferred_element_type=F32
    )
    s = jax.nn.sigmoid(pre)
    hidden = (pre * s).astype(BF16)
    pre_grad = (hidden_grad * s * (1.0 + pre * (1.0 - s))).astype(BF16)
    over_rows = (((0,), (0,)), ((), ()))
    parts = (
        lax.dot_general(agg_ref[:, mine], pre_grad, over_rows, preferred_element_type=F32),
        lax.dot_general(f_ref[...], pre_grad, over_rows, preferred_element_type=F32),
    )
    for k, part in enumerate(parts):
        for j in range(NN):
            g_ref[k * NN + j] = part[:, j * side:(j + 1) * side].astype(BF16)
    part = lax.dot_general(hidden, cot_ref[:, mine], over_rows, preferred_element_type=F32)
    for j in range(NN):
        g_ref[2 * NN + j] = part[j * side:(j + 1) * side, :].astype(BF16)
    out_ref[...] = (
        f_ref[...].astype(F32) + jnp.dot(hidden, ow_ref[:, mine], preferred_element_type=F32)
    ).astype(BF16)


def per_device(
    features,
    tile_blocks,
    tile_rows,
    tile_cols,
    tile_count,
    neighbor_weight,
    root_weight,
    output_weight,
    cotangent,
):
    rows, side = features.shape
    width = NN * side
    quarter = rows // NN
    slots = tile_rows.shape[-1]
    wide = lax.axis_index("wide")
    narrow = lax.axis_index("narrow").astype(I32)
    core = wide % NC
    here = jnp.where(core == 0, (wide // NC) % NY, wide // (NC * NY))

    tiles = tile_blocks[0, 0]
    numbers = jnp.concatenate([tile_rows[0, 0], tile_cols[0, 0], tile_count[0]])
    other_tiles = swap_cores(tiles)
    other_numbers = swap_cores(numbers)

    pieces = call(
        spread_kernel,
        "spread",
        jax.ShapeDtypeStruct((NZ * NN, quarter, side), BF16),
        [HBM],
        VMEM,
        [pltpu.VMEM((rows, side), BF16), pltpu.SemaphoreType.DMA((1,))],
        56,
        10**5,
        10**6,
        features,
    )
    line = exchange(pieces, FIRST)

    weights = call(
        pack_kernel,
        "pack",
        jax.ShapeDtypeStruct((NN, 2 * side + quarter, width), BF16),
        [HBM, HBM, HBM],
        VMEM,
        [
            pltpu.VMEM((side, width), BF16),
            pltpu.VMEM((side, width), BF16),
            pltpu.VMEM((rows, side), BF16),
            pltpu.SemaphoreType.DMA((3,)),
        ],
        56,
        10**5,
        2 * 10**6,
        neighbor_weight,
        root_weight,
        features,
    )
    line, weights, other_numbers = lax.optimization_barrier((line, weights, other_numbers))
    all_weights = exchange(weights, OVER_X)
    by_distance = {0: line}
    for hops in (2, -2, 1, -1):
        by_distance[-hops % NY] = pass_on(line, hops)
    arrived = lax.optimization_barrier([by_distance[d] for d in NEAR[1:]])
    by_distance.update(zip(NEAR[1:], arrived))
    for hops in (1, -1):
        by_distance[-3 * hops % NY] = pass_on(by_distance[-2 * hops % NY], hops)
    by_distance[4] = pass_on(by_distance[6], 2)
    turns = (slots + 2 * STEP - 2) // STEP
    placed = jax.ShapeDtypeStruct((turns * STEP // 2, rows, side), BF16)
    left_own, left_other, meta = call(
        place_kernel,
        "place",
        (placed, placed, jax.ShapeDtypeStruct((2, turns * STEP + 2), I32)),
        [SMEM, SMEM, SMEM, ANY, ANY],
        (VMEM, VMEM, SMEM),
        [
            pltpu.SMEM((turns * STEP,), I32),
            pltpu.VMEM((2, *tiles.shape), BF16),
            pltpu.SemaphoreType.DMA((2,)),
        ],
        10,
        10**7,
        7 * 10**6,
        jnp.concatenate([jnp.stack([core, here]).astype(I32), jnp.array(RING, I32)]),
        numbers,
        other_numbers,
        tiles,
        other_tiles,
    )

    whole = jax.ShapeDtypeStruct((rows, width), F32)
    flops = 2 * slots * rows * quarter * width
    line_size = NZ * NN
    near_own, near_other = call(
        near_kernel,
        "near",
        (whole, whole),
        [SMEM, VMEM, VMEM] + [ANY] * len(NEAR),
        (VMEM, VMEM),
        [
            pltpu.VMEM((len(NEAR) * line_size, quarter, side), BF16),
            pltpu.SemaphoreType.DMA((len(NEAR),)),
        ],
        20,
        flops,
        8 * 10**6,
        meta,
        left_own,
        left_other,
        *[by_distance[d] for d in NEAR],
    )
    part_own, part_other = call(
        far_kernel,
        "far",
        (whole, jax.ShapeDtypeStruct((rows, width), BF16)),
        [SMEM, VMEM, VMEM, VMEM, VMEM] + [ANY] * len(FAR),
        (VMEM, VMEM),
        [
            pltpu.VMEM((rows, width), F32),
            pltpu.VMEM((len(FAR) * line_size, quarter, side), BF16),
            pltpu.SemaphoreType.DMA((len(FAR),)),
        ],
        20,
        flops // 2,
        6 * 10**6,
        meta,
        left_own,
        left_other,
        near_own,
        near_other,
        *[by_distance[d] for d in FAR],
    )
    copies = call(
        join_kernel,
        "join",
        jax.ShapeDtypeStruct((NN, rows, width), BF16),
        [VMEM, VMEM],
        VMEM,
        [],
        8,
        10**6,
        2 * 10**6,
        part_own,
        swap_cores(part_other),
    )
    parts = exchange(copies, OVER_X)

    layer_output, grads = call(
        dense_kernel,
        "dense",
        (
            jax.ShapeDtypeStruct((rows, side), BF16),
            jax.ShapeDtypeStruct((3 * NN, side, side), BF16),
        ),
        [SMEM] + [VMEM] * 5,
        (VMEM, VMEM),
        [pltpu.VMEM((rows, width), BF16)],
        16,
        12 * rows * width * width,
        5 * 10**6,
        narrow[None],
        parts,
        all_weights,
        features,
        cotangent,
        output_weight,
    )

    nearby = len(NEARBY[0])
    chunk = 3 * NN * side // nearby

    def total(pieces, count):
        return call(
            total_kernel,
            "total",
            jax.ShapeDtypeStruct((count, chunk, side), BF16),
            [VMEM],
            VMEM,
            [],
            4,
            10**6,
            10**6,
            pieces,
        )

    summed = total(exchange(grads.reshape(nearby, chunk, side), NEARBY), NY // 2)
    summed = total(exchange(summed, ALONG_Y), NZ // 2)
    summed = total(exchange(summed, ALONG_Z), nearby)
    full = exchange(summed, NEARBY).reshape(3 * NN, side, side)
    return layer_output, *call(
        last_kernel,
        "last",
        (
            jax.ShapeDtypeStruct((side, width), F32),
            jax.ShapeDtypeStruct((side, width), F32),
            jax.ShapeDtypeStruct((width, side), F32),
        ),
        [VMEM],
        (VMEM, VMEM, VMEM),
        [],
        4,
        10**6,
        10**6,
        full,
    )


def solution(mesh):
    return jax.shard_map(
        per_device,
        mesh=mesh,
        in_specs=(
            P("wide", "narrow"),
            P("wide", "narrow", None, None, None),
            P("wide", "narrow", None),
            P("wide", "narrow", None),
            P("wide", "narrow"),
            P("narrow", None),
            P("narrow", None),
            P(),
            P("wide", None),
        ),
        out_specs=(P("wide", "narrow"), P("narrow", None), P("narrow", None), P(None, "narrow")),
        check_vma=False,
    )
```

```python
import jax
import jax.numpy as jnp
from jax import lax
from jax.experimental import pallas as pl
from jax.experimental.pallas import tpu as pltpu
from jax.sharding import PartitionSpec as P

AXES = ("wide", "narrow")
NZ, NY, NC, NN = 8, 8, 2, 4
STEP = 8
VMEM = pl.BlockSpec(memory_space=pltpu.VMEM)
SMEM = pl.BlockSpec(memory_space=pltpu.SMEM)
ANY = pl.BlockSpec(memory_space=pl.ANY)
HBM = pl.BlockSpec(memory_space=pltpu.HBM)
F32, BF16, I32 = jnp.float32, jnp.bfloat16, jnp.int32
NEAR = (0, 6, 2, 7, 1)
FAR = (4, 5, 3)
RING = [(FAR if d in FAR else NEAR).index(d) * NZ * NN for d in range(NY)] + [int(d in FAR) for d in range(NY)]


def places():
    for z in range(NZ):
        for y in range(NY):
            for c in range(NC):
                for n in range(NN):
                    yield z, y, c, n


def device(z, y, c, n):
    return ((z * NY + y) * NC + c) * NN + n


def groups(key):
    found = {}
    for place in places():
        found.setdefault(key(*place), []).append(device(*place))
    return list(found.values())


FIRST = groups(lambda z, y, c, n: (0, y) if c == 0 else (1, z))
OVER_X = groups(lambda z, y, c, n: (z, y, c))
NEARBY = groups(lambda z, y, c, n: (z // 2, y // 2, n))
ALONG_Y = groups(lambda z, y, c, n: (z, y % 2, c, n))
ALONG_Z = groups(lambda z, y, c, n: (z % 2, y, c, n))
OTHER_CORE = [(device(z, y, c, n), device(z, y, 1 - c, n)) for z, y, c, n in places()]


def exchange(pieces, groups_):
    return lax.all_to_all(pieces, AXES, 0, 0, axis_index_groups=groups_, tiled=True)


def swap_cores(value):
    return lax.ppermute(value, AXES, OTHER_CORE)


def pass_on(value, even_hops, odd_hops):
    pairs = []
    for z, y, c, n in places():
        hops = odd_hops if (z if c else y) % 2 else even_hops
        to = (z, (y + hops) % NY, c, n) if c == 0 else ((z + hops) % NZ, y, c, n)
        pairs.append((device(z, y, c, n), device(*to)))
    return lax.ppermute(value, AXES, pairs)


def call(kernel, name, out_shape, in_specs, out_specs, scratch, vmem, flops, size, *args):
    return pl.pallas_call(
        kernel,
        out_shape=out_shape,
        in_specs=in_specs,
        out_specs=out_specs,
        scratch_shapes=scratch,
        compiler_params=pltpu.CompilerParams(vmem_limit_bytes=vmem << 20),
        cost_estimate=pl.CostEstimate(flops=flops, bytes_accessed=size, transcendentals=0),
        name=name,
    )(*args)


def place_kernel(where_ref, own_n_ref, other_n_ref, own_ref, other_ref, lo_ref, lt_ref, meta_ref, order, tiles, sems):
    slots, half = own_ref.shape[0], own_ref.shape[2] // 2
    side = own_ref.shape[1]
    copies = [
        pltpu.make_async_copy(ref, tiles.at[k], sems.at[k]) for k, ref in enumerate((own_ref, other_ref))
    ]
    for copy in copies:
        copy.start()
    room = meta_ref.shape[1] - 2
    first = where_ref[0] == 0
    here = where_ref[1]
    low = lax.broadcasted_iota(I32, own_ref.shape[1:], 1) < half
    for block, (n_ref, l_ref) in enumerate(((own_n_ref, lo_ref), (other_n_ref, lt_ref))):
        count = n_ref[2 * slots]
        for k in range(room):
            order[k] = -1
            meta_ref[block, k] = 0

        def assign(s, carry, block=block, n_ref=n_ref):
            near, far = carry
            col = n_ref[slots + s]
            z, y = lax.shift_right_logical(col, 3), lax.bitwise_and(col, 7)
            ring = jnp.where(first, y, z)
            inner = jnp.where(first, z, y)
            away = lax.bitwise_and(ring - here + NY, NY - 1)
            is_far = where_ref[2 + NY + away]
            at = jnp.where(is_far == 1, room - 1 - far, near)
            order[at] = s
            meta_ref[block, at] = where_ref[2 + away] + inner * NN
            return near + 1 - is_far, far + is_far

        near, far = lax.fori_loop(0, count, assign, (jnp.int32(0), jnp.int32(0)))
        near_turns = lax.shift_right_logical(near + STEP - 1, 3)
        far_turns = lax.shift_right_logical(far + STEP - 1, 3)
        meta_ref[block, room] = near_turns
        meta_ref[block, room + 1] = room // STEP - far_turns

        def one_pair(p, carry, block=block, n_ref=n_ref, l_ref=l_ref):
            slot_a, slot_b = order[2 * p], order[2 * p + 1]
            at_a, at_b = jnp.maximum(slot_a, 0), jnp.maximum(slot_b, 0)
            a, b = tiles[block, at_a].astype(F32), tiles[block, at_b].astype(F32)
            moved = pltpu.roll(jnp.where(first, b, a), half, 1)
            both = jnp.where(low, jnp.where(first, a, moved), jnp.where(first, moved, b))
            row_a = jnp.where(slot_a >= 0, n_ref[at_a], -1)
            row_b = jnp.where(slot_b >= 0, n_ref[at_b], -1)
            rows = jnp.where(low, row_a, row_b)
            for r in range(2):
                l_ref[p, r * side:(r + 1) * side, :] = jnp.where(rows == r, both, 0.0).astype(BF16)
            return carry

        copies[block].wait()
        lax.fori_loop(0, near_turns * (STEP // 2), one_pair, 0)
        lax.fori_loop((room // STEP - far_turns) * (STEP // 2), room // 2, one_pair, 0)


def add_turns(meta_ref, block, first_turn, last_turn, l_ref, blocks, acc):
    def one_turn(i, carry):
        left = jnp.concatenate([l_ref[i * (STEP // 2) + k] for k in range(STEP // 2)], axis=1)
        spots = [meta_ref[block, i * STEP + k] for k in range(STEP)]
        right = jnp.concatenate(
            [jnp.concatenate([blocks[spot + n] for spot in spots], axis=0) for n in range(NN)],
            axis=1,
        )
        acc[...] += jnp.dot(left, right, preferred_element_type=F32)
        return carry

    lax.fori_loop(first_turn, last_turn, one_turn, 0)


def bring(refs, blocks, sems):
    copies, at = [], 0
    for k, ref in enumerate(refs):
        copies.append(
            pltpu.make_async_copy(ref, blocks.at[pl.ds(at, ref.shape[0])], sems.at[k])
        )
        at += ref.shape[0]
    for copy in copies:
        copy.start()
    return copies


def fetch(sources, targets, sems):
    copies = [
        pltpu.make_async_copy(source, target, sems.at[k])
        for k, (source, target) in enumerate(zip(sources, targets))
    ]
    for copy in copies:
        copy.start()
    return copies


def spread_kernel(f_from, out_ref, f_ref, sems):
    for copy in fetch((f_from,), (f_ref,), sems):
        copy.wait()
    quarter = out_ref.shape[1]
    for j in range(out_ref.shape[0]):
        out_ref[j] = f_ref[j % NN * quarter:(j % NN + 1) * quarter, :]


def pack_kernel(nw_from, rw_from, f_from, w_ref, nw_ref, rw_ref, f_ref, sems):
    for copy in fetch((nw_from, rw_from, f_from), (nw_ref, rw_ref, f_ref), sems):
        copy.wait()
    side = nw_ref.shape[0]
    quarter = f_ref.shape[0] // NN
    for j in range(NN):
        w_ref[j, :side, :] = nw_ref[...]
        w_ref[j, side:2 * side, :] = rw_ref[...]
        for q in range(NN):
            w_ref[j, 2 * side:, q * side:(q + 1) * side] = f_ref[q * quarter:(q + 1) * quarter, :]


def near_kernel(meta_ref, lo_ref, lt_ref, *refs):
    *given, po_ref, pt_ref, blocks, sems = refs
    room = meta_ref.shape[1] - 2
    copies = bring(given, blocks, sems)
    po_ref[...] = jnp.zeros_like(po_ref)
    pt_ref[...] = jnp.zeros_like(pt_ref)
    for copy in copies:
        copy.wait()
    add_turns(meta_ref, 1, 0, meta_ref[1, room], lt_ref, blocks, pt_ref)
    add_turns(meta_ref, 0, 0, meta_ref[0, room], lo_ref, blocks, po_ref)


def far_kernel(meta_ref, lo_ref, lt_ref, no_ref, nt_ref, *refs):
    *given, po_ref, pt_ref, acc, blocks, sems = refs
    room = meta_ref.shape[1] - 2
    copies = bring(given, blocks, sems)
    acc[...] = nt_ref[...]
    po_ref[...] = no_ref[...]
    for copy in copies:
        copy.wait()
    add_turns(meta_ref, 1, meta_ref[1, room + 1], room // STEP, lt_ref, blocks, acc)
    pt_ref[...] = acc[...].astype(BF16)
    add_turns(meta_ref, 0, meta_ref[0, room + 1], room // STEP, lo_ref, blocks, po_ref)


def join_kernel(own_ref, came_ref, out_ref):
    joined = (own_ref[...] + came_ref[...].astype(F32)).astype(BF16)
    for j in range(out_ref.shape[0]):
        out_ref[j] = joined


def total_kernel(in_ref, out_ref):
    summed = in_ref[0].astype(F32)
    for j in range(1, in_ref.shape[0]):
        summed = summed + in_ref[j].astype(F32)
    summed = summed.astype(BF16)
    for j in range(out_ref.shape[0]):
        out_ref[j] = summed


def last_kernel(in_ref, neighbor_ref, root_ref, output_ref):
    side = in_ref.shape[1]
    for j in range(NN):
        neighbor_ref[:, j * side:(j + 1) * side] = in_ref[j].astype(F32)
        root_ref[:, j * side:(j + 1) * side] = in_ref[NN + j].astype(F32)
        output_ref[j * side:(j + 1) * side, :] = in_ref[2 * NN + j].astype(F32)


def dense_kernel(n_ref, a_ref, w_ref, f_ref, cot_ref, ow_ref, out_ref, g_ref, agg_ref):
    side = f_ref.shape[1]
    quarter = w_ref.shape[1] - 2 * side
    mine = pl.ds(pl.multiple_of(n_ref[0] * side, side), side)
    root_weight = jnp.concatenate([w_ref[j, side:2 * side, :] for j in range(NN)], axis=0)
    neighbor_weight = jnp.concatenate([w_ref[j, :side, :] for j in range(NN)], axis=0)
    rows = jnp.concatenate(
        [
            jnp.concatenate(
                [w_ref[j, 2 * side:, q * side:(q + 1) * side] for j in range(NN)], axis=1
            )
            for q in range(NN)
        ],
        axis=0,
    )
    agg = a_ref[0].astype(F32)
    for j in range(1, NN):
        agg = agg + a_ref[j].astype(F32)
    agg = agg.astype(BF16)
    agg_ref[...] = agg
    pre = jnp.dot(agg, neighbor_weight, preferred_element_type=F32) + jnp.dot(
        rows, root_weight, preferred_element_type=F32
    )
    hidden_grad = lax.dot_general(
        cot_ref[...], ow_ref[...], (((1,), (1,)), ((), ())), preferred_element_type=F32
    )
    s = jax.nn.sigmoid(pre)
    hidden = (pre * s).astype(BF16)
    pre_grad = (hidden_grad * s * (1.0 + pre * (1.0 - s))).astype(BF16)
    over_rows = (((0,), (0,)), ((), ()))
    parts = (
        lax.dot_general(agg_ref[:, mine], pre_grad, over_rows, preferred_element_type=F32),
        lax.dot_general(f_ref[...], pre_grad, over_rows, preferred_element_type=F32),
    )
    for k, part in enumerate(parts):
        for j in range(NN):
            g_ref[k * NN + j] = part[:, j * side:(j + 1) * side].astype(BF16)
    part = lax.dot_general(hidden, cot_ref[:, mine], over_rows, preferred_element_type=F32)
    for j in range(NN):
        g_ref[2 * NN + j] = part[j * side:(j + 1) * side, :].astype(BF16)
    out_ref[...] = (
        f_ref[...].astype(F32) + jnp.dot(hidden, ow_ref[:, mine], preferred_element_type=F32)
    ).astype(BF16)


def per_device(
    features,
    tile_blocks,
    tile_rows,
    tile_cols,
    tile_count,
    neighbor_weight,
    root_weight,
    output_weight,
    cotangent,
):
    rows, side = features.shape
    width = NN * side
    quarter = rows // NN
    slots = tile_rows.shape[-1]
    wide = lax.axis_index("wide")
    narrow = lax.axis_index("narrow").astype(I32)
    core = wide % NC
    here = jnp.where(core == 0, (wide // NC) % NY, wide // (NC * NY))

    tiles = tile_blocks[0, 0]
    numbers = jnp.concatenate([tile_rows[0, 0], tile_cols[0, 0], tile_count[0]])
    other_tiles = swap_cores(tiles)
    other_numbers = swap_cores(numbers)

    pieces = call(
        spread_kernel,
        "spread",
        jax.ShapeDtypeStruct((NZ * NN, quarter, side), BF16),
        [HBM],
        VMEM,
        [pltpu.VMEM((rows, side), BF16), pltpu.SemaphoreType.DMA((1,))],
        56,
        10**5,
        10**6,
        features,
    )
    line = exchange(pieces, FIRST)

    weights = call(
        pack_kernel,
        "pack",
        jax.ShapeDtypeStruct((NN, 2 * side + quarter, width), BF16),
        [HBM, HBM, HBM],
        VMEM,
        [
            pltpu.VMEM((side, width), BF16),
            pltpu.VMEM((side, width), BF16),
            pltpu.VMEM((rows, side), BF16),
            pltpu.SemaphoreType.DMA((3,)),
        ],
        56,
        10**5,
        2 * 10**6,
        neighbor_weight,
        root_weight,
        features,
    )
    line, weights, other_numbers = lax.optimization_barrier((line, weights, other_numbers))
    all_weights = exchange(weights, OVER_X)
    by_distance = {0: line}
    for hops in (2, -2, 1, -1):
        by_distance[-hops % NY] = pass_on(line, hops, hops)
    across = jnp.where(here % 2 == 0, by_distance[2], by_distance[6])
    arrived, across = lax.optimization_barrier(([by_distance[d] for d in NEAR[1:]], across))
    by_distance.update(zip(NEAR[1:], arrived))
    for hops in (1, -1):
        by_distance[-3 * hops % NY] = pass_on(by_distance[-2 * hops % NY], hops, hops)
    by_distance[4] = pass_on(across, -2, 2)
    turns = (slots + 2 * STEP - 2) // STEP
    placed = jax.ShapeDtypeStruct((turns * STEP // 2, rows, side), BF16)
    left_own, left_other, meta = call(
        place_kernel,
        "place",
        (placed, placed, jax.ShapeDtypeStruct((2, turns * STEP + 2), I32)),
        [SMEM, SMEM, SMEM, ANY, ANY],
        (VMEM, VMEM, SMEM),
        [
            pltpu.SMEM((turns * STEP,), I32),
            pltpu.VMEM((2, *tiles.shape), BF16),
            pltpu.SemaphoreType.DMA((2,)),
        ],
        10,
        10**7,
        7 * 10**6,
        jnp.concatenate([jnp.stack([core, here]).astype(I32), jnp.array(RING, I32)]),
        numbers,
        other_numbers,
        tiles,
        other_tiles,
    )

    whole = jax.ShapeDtypeStruct((rows, width), F32)
    flops = 2 * slots * rows * quarter * width
    line_size = NZ * NN
    near_own, near_other = call(
        near_kernel,
        "near",
        (whole, whole),
        [SMEM, VMEM, VMEM] + [ANY] * len(NEAR),
        (VMEM, VMEM),
        [
            pltpu.VMEM((len(NEAR) * line_size, quarter, side), BF16),
            pltpu.SemaphoreType.DMA((len(NEAR),)),
        ],
        20,
        flops,
        8 * 10**6,
        meta,
        left_own,
        left_other,
        *[by_distance[d] for d in NEAR],
    )
    part_own, part_other = call(
        far_kernel,
        "far",
        (whole, jax.ShapeDtypeStruct((rows, width), BF16)),
        [SMEM, VMEM, VMEM, VMEM, VMEM] + [ANY] * len(FAR),
        (VMEM, VMEM),
        [
            pltpu.VMEM((rows, width), F32),
            pltpu.VMEM((len(FAR) * line_size, quarter, side), BF16),
            pltpu.SemaphoreType.DMA((len(FAR),)),
        ],
        20,
        flops // 2,
        6 * 10**6,
        meta,
        left_own,
        left_other,
        near_own,
        near_other,
        *[by_distance[d] for d in FAR],
    )
    copies = call(
        join_kernel,
        "join",
        jax.ShapeDtypeStruct((NN, rows, width), BF16),
        [VMEM, VMEM],
        VMEM,
        [],
        8,
        10**6,
        2 * 10**6,
        part_own,
        swap_cores(part_other),
    )
    parts = exchange(copies, OVER_X)

    layer_output, grads = call(
        dense_kernel,
        "dense",
        (
            jax.ShapeDtypeStruct((rows, side), BF16),
            jax.ShapeDtypeStruct((3 * NN, side, side), BF16),
        ),
        [SMEM] + [VMEM] * 5,
        (VMEM, VMEM),
        [pltpu.VMEM((rows, width), BF16)],
        16,
        12 * rows * width * width,
        5 * 10**6,
        narrow[None],
        parts,
        all_weights,
        features,
        cotangent,
        output_weight,
    )

    nearby = len(NEARBY[0])
    chunk = 3 * NN * side // nearby

    def total(pieces, count):
        return call(
            total_kernel,
            "total",
            jax.ShapeDtypeStruct((count, chunk, side), BF16),
            [VMEM],
            VMEM,
            [],
            4,
            10**6,
            10**6,
            pieces,
        )

    summed = total(exchange(grads.reshape(nearby, chunk, side), NEARBY), NY // 2)
    summed = total(exchange(summed, ALONG_Y), NZ // 2)
    summed = total(exchange(summed, ALONG_Z), nearby)
    full = exchange(summed, NEARBY).reshape(3 * NN, side, side)
    return layer_output, *call(
        last_kernel,
        "last",
        (
            jax.ShapeDtypeStruct((side, width), F32),
            jax.ShapeDtypeStruct((side, width), F32),
            jax.ShapeDtypeStruct((width, side), F32),
        ),
        [VMEM],
        (VMEM, VMEM, VMEM),
        [],
        4,
        10**6,
        10**6,
        full,
    )


def solution(mesh):
    return jax.shard_map(
        per_device,
        mesh=mesh,
        in_specs=(
            P("wide", "narrow"),
            P("wide", "narrow", None, None, None),
            P("wide", "narrow", None),
            P("wide", "narrow", None),
            P("wide", "narrow"),
            P("narrow", None),
            P("narrow", None),
            P(),
            P("wide", None),
        ),
        out_specs=(P("wide", "narrow"), P("narrow", None), P("narrow", None), P(None, "narrow")),
        check_vma=False,
    )
```

```python
import jax
import jax.numpy as jnp
from jax import lax
from jax.experimental import pallas as pl
from jax.experimental.pallas import tpu as pltpu
from jax.sharding import PartitionSpec as P

AXES = ("wide", "narrow")
NZ, NY, NC, NN = 8, 8, 2, 4
STEP = 8
VMEM = pl.BlockSpec(memory_space=pltpu.VMEM)
SMEM = pl.BlockSpec(memory_space=pltpu.SMEM)
ANY = pl.BlockSpec(memory_space=pl.ANY)
HBM = pl.BlockSpec(memory_space=pltpu.HBM)
F32, BF16, I32 = jnp.float32, jnp.bfloat16, jnp.int32
NEAR = (0, 6, 2, 7, 1)
FAR = (4, 5, 3)
RING = [(FAR if d in FAR else NEAR).index(d) * NZ * NN for d in range(NY)] + [int(d in FAR) for d in range(NY)]


def places():
    for z in range(NZ):
        for y in range(NY):
            for c in range(NC):
                for n in range(NN):
                    yield z, y, c, n


def device(z, y, c, n):
    return ((z * NY + y) * NC + c) * NN + n


def groups(key):
    found = {}
    for place in places():
        found.setdefault(key(*place), []).append(device(*place))
    return list(found.values())


FIRST = groups(lambda z, y, c, n: (0, y) if c == 0 else (1, z))
OVER_X = groups(lambda z, y, c, n: (z, y, c))
NEARBY = groups(lambda z, y, c, n: (z // 2, y // 2, n))
ALONG_Y = groups(lambda z, y, c, n: (z, y % 2, c, n))
ALONG_Z = groups(lambda z, y, c, n: (z % 2, y, c, n))
OTHER_CORE = [(device(z, y, c, n), device(z, y, 1 - c, n)) for z, y, c, n in places()]


def exchange(pieces, groups_):
    return lax.all_to_all(pieces, AXES, 0, 0, axis_index_groups=groups_, tiled=True)


def swap_cores(value):
    return lax.ppermute(value, AXES, OTHER_CORE)


def pass_on(value, even_hops, odd_hops):
    pairs = []
    for z, y, c, n in places():
        hops = odd_hops if (z if c else y) % 2 else even_hops
        to = (z, (y + hops) % NY, c, n) if c == 0 else ((z + hops) % NZ, y, c, n)
        pairs.append((device(z, y, c, n), device(*to)))
    return lax.ppermute(value, AXES, pairs)


def call(kernel, name, out_shape, in_specs, out_specs, scratch, vmem, flops, size, *args):
    return pl.pallas_call(
        kernel,
        out_shape=out_shape,
        in_specs=in_specs,
        out_specs=out_specs,
        scratch_shapes=scratch,
        compiler_params=pltpu.CompilerParams(vmem_limit_bytes=vmem << 20),
        cost_estimate=pl.CostEstimate(flops=flops, bytes_accessed=size, transcendentals=0),
        name=name,
    )(*args)


def place_kernel(where_ref, own_n_ref, other_n_ref, own_ref, other_ref, lo_ref, lt_ref, meta_ref, order, tiles, sems):
    slots, half = own_ref.shape[0], own_ref.shape[2] // 2
    side = own_ref.shape[1]
    copies = [
        pltpu.make_async_copy(ref, tiles.at[k], sems.at[k]) for k, ref in enumerate((own_ref, other_ref))
    ]
    for copy in copies:
        copy.start()
    room = meta_ref.shape[1] - 2
    first = where_ref[0] == 0
    here = where_ref[1]
    low = lax.broadcasted_iota(I32, own_ref.shape[1:], 1) < half
    for block, (n_ref, l_ref) in enumerate(((own_n_ref, lo_ref), (other_n_ref, lt_ref))):
        count = n_ref[2 * slots]
        for k in range(room):
            order[k] = -1
            meta_ref[block, k] = 0

        def assign(s, carry, block=block, n_ref=n_ref):
            near, far = carry
            col = n_ref[slots + s]
            z, y = lax.shift_right_logical(col, 3), lax.bitwise_and(col, 7)
            ring = jnp.where(first, y, z)
            inner = jnp.where(first, z, y)
            away = lax.bitwise_and(ring - here + NY, NY - 1)
            is_far = where_ref[2 + NY + away]
            at = jnp.where(is_far == 1, room - 1 - far, near)
            order[at] = s
            meta_ref[block, at] = where_ref[2 + away] + inner * NN
            return near + 1 - is_far, far + is_far

        near, far = lax.fori_loop(0, count, assign, (jnp.int32(0), jnp.int32(0)))
        near_turns = lax.shift_right_logical(near + STEP - 1, 3)
        far_turns = lax.shift_right_logical(far + STEP - 1, 3)
        meta_ref[block, room] = near_turns
        meta_ref[block, room + 1] = room // STEP - far_turns

        def one_pair(p, carry, block=block, n_ref=n_ref, l_ref=l_ref):
            slot_a, slot_b = order[2 * p], order[2 * p + 1]
            at_a, at_b = jnp.maximum(slot_a, 0), jnp.maximum(slot_b, 0)
            a, b = tiles[block, at_a].astype(F32), tiles[block, at_b].astype(F32)
            moved = pltpu.roll(jnp.where(first, b, a), half, 1)
            both = jnp.where(low, jnp.where(first, a, moved), jnp.where(first, moved, b))
            row_a = jnp.where(slot_a >= 0, n_ref[at_a], -1)
            row_b = jnp.where(slot_b >= 0, n_ref[at_b], -1)
            rows = jnp.where(low, row_a, row_b)
            for r in range(2):
                l_ref[p, r * side:(r + 1) * side, :] = jnp.where(rows == r, both, 0.0).astype(BF16)
            return carry

        copies[block].wait()
        lax.fori_loop(0, near_turns * (STEP // 2), one_pair, 0)
        lax.fori_loop((room // STEP - far_turns) * (STEP // 2), room // 2, one_pair, 0)


def add_turns(meta_ref, block, first_turn, last_turn, l_ref, blocks, acc):
    def one_turn(i, carry):
        left = jnp.concatenate([l_ref[i * (STEP // 2) + k] for k in range(STEP // 2)], axis=1)
        spots = [meta_ref[block, i * STEP + k] for k in range(STEP)]
        right = jnp.concatenate(
            [jnp.concatenate([blocks[spot + n] for spot in spots], axis=0) for n in range(NN)],
            axis=1,
        )
        acc[...] += jnp.dot(left, right, preferred_element_type=F32)
        return carry

    lax.fori_loop(first_turn, last_turn, one_turn, 0)


def bring(refs, blocks, sems):
    copies, at = [], 0
    for k, ref in enumerate(refs):
        copies.append(
            pltpu.make_async_copy(ref, blocks.at[pl.ds(at, ref.shape[0])], sems.at[k])
        )
        at += ref.shape[0]
    for copy in copies:
        copy.start()
    return copies


def fetch(sources, targets, sems):
    copies = [
        pltpu.make_async_copy(source, target, sems.at[k])
        for k, (source, target) in enumerate(zip(sources, targets))
    ]
    for copy in copies:
        copy.start()
    return copies


def spread_kernel(f_from, out_ref, f_ref, sems):
    for copy in fetch((f_from,), (f_ref,), sems):
        copy.wait()
    quarter = out_ref.shape[1]
    for j in range(out_ref.shape[0]):
        out_ref[j] = f_ref[j % NN * quarter:(j % NN + 1) * quarter, :]


def pack_kernel(nw_from, rw_from, f_from, w_ref, nw_ref, rw_ref, f_ref, sems):
    for copy in fetch((nw_from, rw_from, f_from), (nw_ref, rw_ref, f_ref), sems):
        copy.wait()
    side = nw_ref.shape[0]
    quarter = f_ref.shape[0] // NN
    for j in range(NN):
        w_ref[j, :side, :] = nw_ref[...]
        w_ref[j, side:2 * side, :] = rw_ref[...]
        for q in range(NN):
            w_ref[j, 2 * side:, q * side:(q + 1) * side] = f_ref[q * quarter:(q + 1) * quarter, :]


def near_kernel(meta_ref, lo_ref, lt_ref, *refs):
    *given, po_ref, pt_ref, blocks, sems = refs
    room = meta_ref.shape[1] - 2
    copies = bring(given, blocks, sems)
    po_ref[...] = jnp.zeros_like(po_ref)
    pt_ref[...] = jnp.zeros_like(pt_ref)
    for copy in copies:
        copy.wait()
    add_turns(meta_ref, 1, 0, meta_ref[1, room], lt_ref, blocks, pt_ref)
    add_turns(meta_ref, 0, 0, meta_ref[0, room], lo_ref, blocks, po_ref)


def far_kernel(meta_ref, lo_ref, lt_ref, no_ref, nt_ref, *refs):
    *given, po_ref, pt_ref, acc, blocks, sems = refs
    room = meta_ref.shape[1] - 2
    copies = bring(given, blocks, sems)
    acc[...] = nt_ref[...]
    po_ref[...] = no_ref[...]
    for copy in copies:
        copy.wait()
    add_turns(meta_ref, 1, meta_ref[1, room + 1], room // STEP, lt_ref, blocks, acc)
    pt_ref[...] = acc[...].astype(BF16)
    add_turns(meta_ref, 0, meta_ref[0, room + 1], room // STEP, lo_ref, blocks, po_ref)


def join_kernel(own_ref, came_ref, out_ref):
    joined = (own_ref[...] + came_ref[...].astype(F32)).astype(BF16)
    for j in range(out_ref.shape[0]):
        out_ref[j] = joined


def total_kernel(in_ref, out_ref):
    summed = in_ref[0].astype(F32)
    for j in range(1, in_ref.shape[0]):
        summed = summed + in_ref[j].astype(F32)
    summed = summed.astype(BF16)
    for j in range(out_ref.shape[0]):
        out_ref[j] = summed


def last_kernel(in_ref, neighbor_ref, root_ref, output_ref):
    side = in_ref.shape[1]
    for j in range(NN):
        neighbor_ref[:, j * side:(j + 1) * side] = in_ref[j].astype(F32)
        root_ref[:, j * side:(j + 1) * side] = in_ref[NN + j].astype(F32)
        output_ref[j * side:(j + 1) * side, :] = in_ref[2 * NN + j].astype(F32)


def dense_kernel(n_ref, a_ref, w_ref, f_ref, cot_ref, ow_ref, out_ref, g_ref, agg_ref):
    side = f_ref.shape[1]
    quarter = w_ref.shape[1] - 2 * side
    mine = pl.ds(pl.multiple_of(n_ref[0] * side, side), side)
    root_weight = jnp.concatenate([w_ref[j, side:2 * side, :] for j in range(NN)], axis=0)
    neighbor_weight = jnp.concatenate([w_ref[j, :side, :] for j in range(NN)], axis=0)
    rows = jnp.concatenate(
        [
            jnp.concatenate(
                [w_ref[j, 2 * side:, q * side:(q + 1) * side] for j in range(NN)], axis=1
            )
            for q in range(NN)
        ],
        axis=0,
    )
    agg = a_ref[0].astype(F32)
    for j in range(1, NN):
        agg = agg + a_ref[j].astype(F32)
    agg = agg.astype(BF16)
    agg_ref[...] = agg
    pre = jnp.dot(agg, neighbor_weight, preferred_element_type=F32) + jnp.dot(
        rows, root_weight, preferred_element_type=F32
    )
    hidden_grad = lax.dot_general(
        cot_ref[...], ow_ref[...], (((1,), (1,)), ((), ())), preferred_element_type=F32
    )
    s = jax.nn.sigmoid(pre)
    hidden = (pre * s).astype(BF16)
    pre_grad = (hidden_grad * s * (1.0 + pre * (1.0 - s))).astype(BF16)
    over_rows = (((0,), (0,)), ((), ()))
    parts = (
        lax.dot_general(agg_ref[:, mine], pre_grad, over_rows, preferred_element_type=F32),
        lax.dot_general(f_ref[...], pre_grad, over_rows, preferred_element_type=F32),
    )
    for k, part in enumerate(parts):
        for j in range(NN):
            g_ref[k * NN + j] = part[:, j * side:(j + 1) * side].astype(BF16)
    part = lax.dot_general(hidden, cot_ref[:, mine], over_rows, preferred_element_type=F32)
    for j in range(NN):
        g_ref[2 * NN + j] = part[j * side:(j + 1) * side, :].astype(BF16)
    out_ref[...] = (
        f_ref[...].astype(F32) + jnp.dot(hidden, ow_ref[:, mine], preferred_element_type=F32)
    ).astype(BF16)


def per_device(
    features,
    tile_blocks,
    tile_rows,
    tile_cols,
    tile_count,
    neighbor_weight,
    root_weight,
    output_weight,
    cotangent,
):
    rows, side = features.shape
    width = NN * side
    quarter = rows // NN
    slots = tile_rows.shape[-1]
    wide = lax.axis_index("wide")
    narrow = lax.axis_index("narrow").astype(I32)
    core = wide % NC
    here = jnp.where(core == 0, (wide // NC) % NY, wide // (NC * NY))

    tiles = tile_blocks[0, 0]
    numbers = jnp.concatenate([tile_rows[0, 0], tile_cols[0, 0], tile_count[0]])
    other_tiles = swap_cores(tiles)
    other_numbers = swap_cores(numbers)

    pieces = call(
        spread_kernel,
        "spread",
        jax.ShapeDtypeStruct((NZ * NN, quarter, side), BF16),
        [HBM],
        VMEM,
        [pltpu.VMEM((rows, side), BF16), pltpu.SemaphoreType.DMA((1,))],
        56,
        10**5,
        10**6,
        features,
    )
    line = exchange(pieces, FIRST)

    weights = call(
        pack_kernel,
        "pack",
        jax.ShapeDtypeStruct((NN, 2 * side + quarter, width), BF16),
        [HBM, HBM, HBM],
        VMEM,
        [
            pltpu.VMEM((side, width), BF16),
            pltpu.VMEM((side, width), BF16),
            pltpu.VMEM((rows, side), BF16),
            pltpu.SemaphoreType.DMA((3,)),
        ],
        56,
        10**5,
        2 * 10**6,
        neighbor_weight,
        root_weight,
        features,
    )
    line, weights, other_numbers = lax.optimization_barrier((line, weights, other_numbers))
    all_weights = exchange(weights, OVER_X)
    by_distance = {0: line}
    for hops in (2, -2, 1, -1):
        by_distance[-hops % NY] = pass_on(line, hops, hops)
    turns = (slots + 2 * STEP - 2) // STEP
    placed = jax.ShapeDtypeStruct((turns * STEP // 2, rows, side), BF16)
    left_own, left_other, meta = call(
        place_kernel,
        "place",
        (placed, placed, jax.ShapeDtypeStruct((2, turns * STEP + 2), I32)),
        [SMEM, SMEM, SMEM, ANY, ANY],
        (VMEM, VMEM, SMEM),
        [
            pltpu.SMEM((turns * STEP,), I32),
            pltpu.VMEM((2, *tiles.shape), BF16),
            pltpu.SemaphoreType.DMA((2,)),
        ],
        10,
        10**7,
        7 * 10**6,
        jnp.concatenate([jnp.stack([core, here]).astype(I32), jnp.array(RING, I32)]),
        numbers,
        other_numbers,
        tiles,
        other_tiles,
    )

    across = jnp.where(here % 2 == 0, by_distance[2], by_distance[6])
    arrived, across, meta = lax.optimization_barrier(([by_distance[d] for d in NEAR[1:]], across, meta))
    by_distance.update(zip(NEAR[1:], arrived))
    for hops in (1, -1):
        by_distance[-3 * hops % NY] = pass_on(by_distance[-2 * hops % NY], hops, hops)
    by_distance[4] = pass_on(across, -2, 2)
    whole = jax.ShapeDtypeStruct((rows, width), F32)
    flops = 2 * slots * rows * quarter * width
    line_size = NZ * NN
    near_own, near_other = call(
        near_kernel,
        "near",
        (whole, whole),
        [SMEM, VMEM, VMEM] + [ANY] * len(NEAR),
        (VMEM, VMEM),
        [
            pltpu.VMEM((len(NEAR) * line_size, quarter, side), BF16),
            pltpu.SemaphoreType.DMA((len(NEAR),)),
        ],
        20,
        flops,
        8 * 10**6,
        meta,
        left_own,
        left_other,
        *[by_distance[d] for d in NEAR],
    )
    part_own, part_other = call(
        far_kernel,
        "far",
        (whole, jax.ShapeDtypeStruct((rows, width), BF16)),
        [SMEM, VMEM, VMEM, VMEM, VMEM] + [ANY] * len(FAR),
        (VMEM, VMEM),
        [
            pltpu.VMEM((rows, width), F32),
            pltpu.VMEM((len(FAR) * line_size, quarter, side), BF16),
            pltpu.SemaphoreType.DMA((len(FAR),)),
        ],
        20,
        flops // 2,
        6 * 10**6,
        meta,
        left_own,
        left_other,
        near_own,
        near_other,
        *[by_distance[d] for d in FAR],
    )
    copies = call(
        join_kernel,
        "join",
        jax.ShapeDtypeStruct((NN, rows, width), BF16),
        [VMEM, VMEM],
        VMEM,
        [],
        8,
        10**6,
        2 * 10**6,
        part_own,
        swap_cores(part_other),
    )
    parts = exchange(copies, OVER_X)

    layer_output, grads = call(
        dense_kernel,
        "dense",
        (
            jax.ShapeDtypeStruct((rows, side), BF16),
            jax.ShapeDtypeStruct((3 * NN, side, side), BF16),
        ),
        [SMEM] + [VMEM] * 5,
        (VMEM, VMEM),
        [pltpu.VMEM((rows, width), BF16)],
        16,
        12 * rows * width * width,
        5 * 10**6,
        narrow[None],
        parts,
        all_weights,
        features,
        cotangent,
        output_weight,
    )

    nearby = len(NEARBY[0])
    chunk = 3 * NN * side // nearby

    def total(pieces, count):
        return call(
            total_kernel,
            "total",
            jax.ShapeDtypeStruct((count, chunk, side), BF16),
            [VMEM],
            VMEM,
            [],
            4,
            10**6,
            10**6,
            pieces,
        )

    summed = total(exchange(grads.reshape(nearby, chunk, side), NEARBY), NY // 2)
    summed = total(exchange(summed, ALONG_Y), NZ // 2)
    summed = total(exchange(summed, ALONG_Z), nearby)
    full = exchange(summed, NEARBY).reshape(3 * NN, side, side)
    return layer_output, *call(
        last_kernel,
        "last",
        (
            jax.ShapeDtypeStruct((side, width), F32),
            jax.ShapeDtypeStruct((side, width), F32),
            jax.ShapeDtypeStruct((width, side), F32),
        ),
        [VMEM],
        (VMEM, VMEM, VMEM),
        [],
        4,
        10**6,
        10**6,
        full,
    )


def solution(mesh):
    return jax.shard_map(
        per_device,
        mesh=mesh,
        in_specs=(
            P("wide", "narrow"),
            P("wide", "narrow", None, None, None),
            P("wide", "narrow", None),
            P("wide", "narrow", None),
            P("wide", "narrow"),
            P("narrow", None),
            P("narrow", None),
            P(),
            P("wide", None),
        ),
        out_specs=(P("wide", "narrow"), P("narrow", None), P("narrow", None), P(None, "narrow")),
        check_vma=False,
    )
```

```python
import jax
import jax.numpy as jnp
from jax import lax
from jax.experimental import pallas as pl
from jax.experimental.pallas import tpu as pltpu
from jax.sharding import PartitionSpec as P

AXES = ("wide", "narrow")
NZ, NY, NC, NN = 8, 8, 2, 4
STEP = 8
VMEM = pl.BlockSpec(memory_space=pltpu.VMEM)
SMEM = pl.BlockSpec(memory_space=pltpu.SMEM)
ANY = pl.BlockSpec(memory_space=pl.ANY)
HBM = pl.BlockSpec(memory_space=pltpu.HBM)
F32, BF16, I32 = jnp.float32, jnp.bfloat16, jnp.int32
NEAR = (0, 6, 2, 7, 1)
FAR = (4, 5, 3)
RING = [(FAR if d in FAR else NEAR).index(d) * NZ * NN for d in range(NY)] + [int(d in FAR) for d in range(NY)]


def places():
    for z in range(NZ):
        for y in range(NY):
            for c in range(NC):
                for n in range(NN):
                    yield z, y, c, n


def device(z, y, c, n):
    return ((z * NY + y) * NC + c) * NN + n


def groups(key):
    found = {}
    for place in places():
        found.setdefault(key(*place), []).append(device(*place))
    return list(found.values())


FIRST = groups(lambda z, y, c, n: (0, y) if c == 0 else (1, z))
OVER_X = groups(lambda z, y, c, n: (z, y, c))
NEARBY = groups(lambda z, y, c, n: (z // 2, y // 2, n))
ALONG_Y = groups(lambda z, y, c, n: (z, y % 2, c, n))
ALONG_Z = groups(lambda z, y, c, n: (z % 2, y, c, n))
OTHER_CORE = [(device(z, y, c, n), device(z, y, 1 - c, n)) for z, y, c, n in places()]


def exchange(pieces, groups_):
    return lax.all_to_all(pieces, AXES, 0, 0, axis_index_groups=groups_, tiled=True)


def swap_cores(value):
    return lax.ppermute(value, AXES, OTHER_CORE)


def pass_on(value, even_hops, odd_hops):
    pairs = []
    for z, y, c, n in places():
        hops = odd_hops if (z if c else y) % 2 else even_hops
        to = (z, (y + hops) % NY, c, n) if c == 0 else ((z + hops) % NZ, y, c, n)
        pairs.append((device(z, y, c, n), device(*to)))
    return lax.ppermute(value, AXES, pairs)


def call(kernel, name, out_shape, in_specs, out_specs, scratch, vmem, flops, size, *args):
    return pl.pallas_call(
        kernel,
        out_shape=out_shape,
        in_specs=in_specs,
        out_specs=out_specs,
        scratch_shapes=scratch,
        compiler_params=pltpu.CompilerParams(vmem_limit_bytes=vmem << 20),
        cost_estimate=pl.CostEstimate(flops=flops, bytes_accessed=size, transcendentals=0),
        name=name,
    )(*args)


def place_kernel(where_ref, own_n_ref, other_n_ref, own_ref, other_ref, lo_ref, lt_ref, meta_ref, order, tiles, sems):
    slots, half = own_ref.shape[0], own_ref.shape[2] // 2
    side = own_ref.shape[1]
    copies = [
        pltpu.make_async_copy(ref, tiles.at[k], sems.at[k]) for k, ref in enumerate((own_ref, other_ref))
    ]
    for copy in copies:
        copy.start()
    room = meta_ref.shape[1] - 2
    first = where_ref[0] == 0
    here = where_ref[1]
    low = lax.broadcasted_iota(I32, own_ref.shape[1:], 1) < half
    for block, (n_ref, l_ref) in enumerate(((own_n_ref, lo_ref), (other_n_ref, lt_ref))):
        count = n_ref[2 * slots]
        for k in range(room):
            order[k] = -1
            meta_ref[block, k] = 0

        def assign(s, carry, block=block, n_ref=n_ref):
            near, far = carry
            col = n_ref[slots + s]
            z, y = lax.shift_right_logical(col, 3), lax.bitwise_and(col, 7)
            ring = jnp.where(first, y, z)
            inner = jnp.where(first, z, y)
            away = lax.bitwise_and(ring - here + NY, NY - 1)
            is_far = where_ref[2 + NY + away]
            at = jnp.where(is_far == 1, room - 1 - far, near)
            order[at] = s
            meta_ref[block, at] = where_ref[2 + away] + inner * NN
            return near + 1 - is_far, far + is_far

        near, far = lax.fori_loop(0, count, assign, (jnp.int32(0), jnp.int32(0)))
        near_turns = lax.shift_right_logical(near + STEP - 1, 3)
        far_turns = lax.shift_right_logical(far + STEP - 1, 3)
        meta_ref[block, room] = near_turns
        meta_ref[block, room + 1] = room // STEP - far_turns

        def one_pair(p, carry, block=block, n_ref=n_ref, l_ref=l_ref):
            slot_a, slot_b = order[2 * p], order[2 * p + 1]
            at_a, at_b = jnp.maximum(slot_a, 0), jnp.maximum(slot_b, 0)
            a, b = tiles[block, at_a].astype(F32), tiles[block, at_b].astype(F32)
            moved = pltpu.roll(jnp.where(first, b, a), half, 1)
            both = jnp.where(low, jnp.where(first, a, moved), jnp.where(first, moved, b))
            row_a = jnp.where(slot_a >= 0, n_ref[at_a], -1)
            row_b = jnp.where(slot_b >= 0, n_ref[at_b], -1)
            rows = jnp.where(low, row_a, row_b)
            for r in range(2):
                l_ref[p, r * side:(r + 1) * side, :] = jnp.where(rows == r, both, 0.0).astype(BF16)
            return carry

        copies[block].wait()
        lax.fori_loop(0, near_turns * (STEP // 2), one_pair, 0)
        lax.fori_loop((room // STEP - far_turns) * (STEP // 2), room // 2, one_pair, 0)


def add_turns(meta_ref, block, first_turn, last_turn, l_ref, blocks, acc):
    def one_turn(i, carry):
        left = jnp.concatenate([l_ref[i * (STEP // 2) + k] for k in range(STEP // 2)], axis=1)
        spots = [meta_ref[block, i * STEP + k] for k in range(STEP)]
        right = jnp.concatenate(
            [jnp.concatenate([blocks[spot + n] for spot in spots], axis=0) for n in range(NN)],
            axis=1,
        )
        acc[...] += jnp.dot(left, right, preferred_element_type=F32)
        return carry

    lax.fori_loop(first_turn, last_turn, one_turn, 0)


def bring(refs, blocks, sems):
    copies, at = [], 0
    for k, ref in enumerate(refs):
        copies.append(
            pltpu.make_async_copy(ref, blocks.at[pl.ds(at, ref.shape[0])], sems.at[k])
        )
        at += ref.shape[0]
    for copy in copies:
        copy.start()
    return copies


def fetch(sources, targets, sems):
    copies = [
        pltpu.make_async_copy(source, target, sems.at[k])
        for k, (source, target) in enumerate(zip(sources, targets))
    ]
    for copy in copies:
        copy.start()
    return copies


def spread_kernel(f_from, out_ref, f_ref, sems):
    for copy in fetch((f_from,), (f_ref,), sems):
        copy.wait()
    quarter = out_ref.shape[1]
    for j in range(out_ref.shape[0]):
        out_ref[j] = f_ref[j % NN * quarter:(j % NN + 1) * quarter, :]


def pack_kernel(nw_from, rw_from, f_from, w_ref, nw_ref, rw_ref, f_ref, sems):
    for copy in fetch((nw_from, rw_from, f_from), (nw_ref, rw_ref, f_ref), sems):
        copy.wait()
    side = nw_ref.shape[0]
    quarter = f_ref.shape[0] // NN
    for j in range(NN):
        w_ref[j, :side, :] = nw_ref[...]
        w_ref[j, side:2 * side, :] = rw_ref[...]
        for q in range(NN):
            w_ref[j, 2 * side:, q * side:(q + 1) * side] = f_ref[q * quarter:(q + 1) * quarter, :]


def near_kernel(meta_ref, lo_ref, lt_ref, *refs):
    *given, po_ref, pt_ref, blocks, sems = refs
    room = meta_ref.shape[1] - 2
    copies = bring(given, blocks, sems)
    po_ref[...] = jnp.zeros_like(po_ref)
    pt_ref[...] = jnp.zeros_like(pt_ref)
    for copy in copies:
        copy.wait()
    add_turns(meta_ref, 1, 0, meta_ref[1, room], lt_ref, blocks, pt_ref)
    add_turns(meta_ref, 0, 0, meta_ref[0, room], lo_ref, blocks, po_ref)


def far_kernel(meta_ref, lo_ref, lt_ref, no_ref, nt_ref, *refs):
    *given, po_ref, pt_ref, acc, blocks, sems = refs
    room = meta_ref.shape[1] - 2
    copies = bring(given, blocks, sems)
    acc[...] = nt_ref[...]
    po_ref[...] = no_ref[...]
    for copy in copies:
        copy.wait()
    add_turns(meta_ref, 1, meta_ref[1, room + 1], room // STEP, lt_ref, blocks, acc)
    pt_ref[...] = acc[...].astype(BF16)
    add_turns(meta_ref, 0, meta_ref[0, room + 1], room // STEP, lo_ref, blocks, po_ref)


def join_kernel(own_ref, came_ref, out_ref):
    joined = (own_ref[...] + came_ref[...].astype(F32)).astype(BF16)
    for j in range(out_ref.shape[0]):
        out_ref[j] = joined


def total_kernel(in_ref, out_ref):
    summed = in_ref[0].astype(F32)
    for j in range(1, in_ref.shape[0]):
        summed = summed + in_ref[j].astype(F32)
    summed = summed.astype(BF16)
    for j in range(out_ref.shape[0]):
        out_ref[j] = summed


def last_kernel(in_ref, neighbor_ref, root_ref, output_ref):
    side = in_ref.shape[1]
    for j in range(NN):
        neighbor_ref[:, j * side:(j + 1) * side] = in_ref[j].astype(F32)
        root_ref[:, j * side:(j + 1) * side] = in_ref[NN + j].astype(F32)
        output_ref[j * side:(j + 1) * side, :] = in_ref[2 * NN + j].astype(F32)


def dense_kernel(n_ref, a_ref, w_ref, f_ref, cot_ref, ow_ref, out_ref, g_ref, agg_ref):
    side = f_ref.shape[1]
    quarter = w_ref.shape[1] - 2 * side
    mine = pl.ds(pl.multiple_of(n_ref[0] * side, side), side)
    root_weight = jnp.concatenate([w_ref[j, side:2 * side, :] for j in range(NN)], axis=0)
    neighbor_weight = jnp.concatenate([w_ref[j, :side, :] for j in range(NN)], axis=0)
    rows = jnp.concatenate(
        [
            jnp.concatenate(
                [w_ref[j, 2 * side:, q * side:(q + 1) * side] for j in range(NN)], axis=1
            )
            for q in range(NN)
        ],
        axis=0,
    )
    agg = a_ref[0].astype(F32)
    for j in range(1, NN):
        agg = agg + a_ref[j].astype(F32)
    agg = agg.astype(BF16)
    agg_ref[...] = agg
    pre = jnp.dot(agg, neighbor_weight, preferred_element_type=F32) + jnp.dot(
        rows, root_weight, preferred_element_type=F32
    )
    hidden_grad = lax.dot_general(
        cot_ref[...], ow_ref[...], (((1,), (1,)), ((), ())), preferred_element_type=F32
    )
    s = jax.nn.sigmoid(pre)
    hidden = (pre * s).astype(BF16)
    pre_grad = (hidden_grad * s * (1.0 + pre * (1.0 - s))).astype(BF16)
    over_rows = (((0,), (0,)), ((), ()))
    parts = (
        lax.dot_general(agg_ref[:, mine], pre_grad, over_rows, preferred_element_type=F32),
        lax.dot_general(f_ref[...], pre_grad, over_rows, preferred_element_type=F32),
    )
    for k, part in enumerate(parts):
        for j in range(NN):
            g_ref[k * NN + j] = part[:, j * side:(j + 1) * side].astype(BF16)
    part = lax.dot_general(hidden, cot_ref[:, mine], over_rows, preferred_element_type=F32)
    for j in range(NN):
        g_ref[2 * NN + j] = part[j * side:(j + 1) * side, :].astype(BF16)
    out_ref[...] = (
        f_ref[...].astype(F32) + jnp.dot(hidden, ow_ref[:, mine], preferred_element_type=F32)
    ).astype(BF16)


def per_device(
    features,
    tile_blocks,
    tile_rows,
    tile_cols,
    tile_count,
    neighbor_weight,
    root_weight,
    output_weight,
    cotangent,
):
    rows, side = features.shape
    width = NN * side
    quarter = rows // NN
    slots = tile_rows.shape[-1]
    wide = lax.axis_index("wide")
    narrow = lax.axis_index("narrow").astype(I32)
    core = wide % NC
    here = jnp.where(core == 0, (wide // NC) % NY, wide // (NC * NY))

    tiles = tile_blocks[0, 0]
    numbers = jnp.concatenate([tile_rows[0, 0], tile_cols[0, 0], tile_count[0]])
    other_tiles = swap_cores(tiles)
    other_numbers = swap_cores(numbers)

    pieces = call(
        spread_kernel,
        "spread",
        jax.ShapeDtypeStruct((NZ * NN, quarter, side), BF16),
        [HBM],
        VMEM,
        [pltpu.VMEM((rows, side), BF16), pltpu.SemaphoreType.DMA((1,))],
        56,
        10**5,
        10**6,
        features,
    )
    line = exchange(pieces, FIRST)

    weights = call(
        pack_kernel,
        "pack",
        jax.ShapeDtypeStruct((NN, 2 * side + quarter, width), BF16),
        [HBM, HBM, HBM],
        VMEM,
        [
            pltpu.VMEM((side, width), BF16),
            pltpu.VMEM((side, width), BF16),
            pltpu.VMEM((rows, side), BF16),
            pltpu.SemaphoreType.DMA((3,)),
        ],
        56,
        10**5,
        2 * 10**6,
        neighbor_weight,
        root_weight,
        features,
    )
    line, weights, other_numbers = lax.optimization_barrier((line, weights, other_numbers))
    all_weights = exchange(weights, OVER_X)
    by_distance = {0: line}
    for hops in (2, -2, 1, -1):
        by_distance[-hops % NY] = pass_on(line, hops, hops)
    turns = (slots + 2 * STEP - 2) // STEP
    placed = jax.ShapeDtypeStruct((turns * STEP // 2, rows, side), BF16)
    left_own, left_other, meta = call(
        place_kernel,
        "place",
        (placed, placed, jax.ShapeDtypeStruct((2, turns * STEP + 2), I32)),
        [SMEM, SMEM, SMEM, ANY, ANY],
        (VMEM, VMEM, SMEM),
        [
            pltpu.SMEM((turns * STEP,), I32),
            pltpu.VMEM((2, *tiles.shape), BF16),
            pltpu.SemaphoreType.DMA((2,)),
        ],
        10,
        10**7,
        7 * 10**6,
        jnp.concatenate([jnp.stack([core, here]).astype(I32), jnp.array(RING, I32)]),
        numbers,
        other_numbers,
        tiles,
        other_tiles,
    )

    across = jnp.where(here % 2 == 0, by_distance[2], by_distance[6])
    arrived, across = lax.optimization_barrier(([by_distance[d] for d in NEAR[1:3]], across))
    by_distance.update(zip(NEAR[1:3], arrived))
    for hops in (1, -1):
        by_distance[-3 * hops % NY] = pass_on(by_distance[-2 * hops % NY], hops, hops)
    by_distance[4] = pass_on(across, -2, 2)
    whole = jax.ShapeDtypeStruct((rows, width), F32)
    flops = 2 * slots * rows * quarter * width
    line_size = NZ * NN
    near_own, near_other = call(
        near_kernel,
        "near",
        (whole, whole),
        [SMEM, VMEM, VMEM] + [ANY] * len(NEAR),
        (VMEM, VMEM),
        [
            pltpu.VMEM((len(NEAR) * line_size, quarter, side), BF16),
            pltpu.SemaphoreType.DMA((len(NEAR),)),
        ],
        20,
        flops,
        8 * 10**6,
        meta,
        left_own,
        left_other,
        *[by_distance[d] for d in NEAR],
    )
    part_own, part_other = call(
        far_kernel,
        "far",
        (whole, jax.ShapeDtypeStruct((rows, width), BF16)),
        [SMEM, VMEM, VMEM, VMEM, VMEM] + [ANY] * len(FAR),
        (VMEM, VMEM),
        [
            pltpu.VMEM((rows, width), F32),
            pltpu.VMEM((len(FAR) * line_size, quarter, side), BF16),
            pltpu.SemaphoreType.DMA((len(FAR),)),
        ],
        20,
        flops // 2,
        6 * 10**6,
        meta,
        left_own,
        left_other,
        near_own,
        near_other,
        *[by_distance[d] for d in FAR],
    )
    copies = call(
        join_kernel,
        "join",
        jax.ShapeDtypeStruct((NN, rows, width), BF16),
        [VMEM, VMEM],
        VMEM,
        [],
        8,
        10**6,
        2 * 10**6,
        part_own,
        swap_cores(part_other),
    )
    parts = exchange(copies, OVER_X)

    layer_output, grads = call(
        dense_kernel,
        "dense",
        (
            jax.ShapeDtypeStruct((rows, side), BF16),
            jax.ShapeDtypeStruct((3 * NN, side, side), BF16),
        ),
        [SMEM] + [VMEM] * 5,
        (VMEM, VMEM),
        [pltpu.VMEM((rows, width), BF16)],
        16,
        12 * rows * width * width,
        5 * 10**6,
        narrow[None],
        parts,
        all_weights,
        features,
        cotangent,
        output_weight,
    )

    nearby = len(NEARBY[0])
    chunk = 3 * NN * side // nearby

    def total(pieces, count):
        return call(
            total_kernel,
            "total",
            jax.ShapeDtypeStruct((count, chunk, side), BF16),
            [VMEM],
            VMEM,
            [],
            4,
            10**6,
            10**6,
            pieces,
        )

    summed = total(exchange(grads.reshape(nearby, chunk, side), NEARBY), NY // 2)
    summed = total(exchange(summed, ALONG_Y), NZ // 2)
    summed = total(exchange(summed, ALONG_Z), nearby)
    full = exchange(summed, NEARBY).reshape(3 * NN, side, side)
    return layer_output, *call(
        last_kernel,
        "last",
        (
            jax.ShapeDtypeStruct((side, width), F32),
            jax.ShapeDtypeStruct((side, width), F32),
            jax.ShapeDtypeStruct((width, side), F32),
        ),
        [VMEM],
        (VMEM, VMEM, VMEM),
        [],
        4,
        10**6,
        10**6,
        full,
    )


def solution(mesh):
    return jax.shard_map(
        per_device,
        mesh=mesh,
        in_specs=(
            P("wide", "narrow"),
            P("wide", "narrow", None, None, None),
            P("wide", "narrow", None),
            P("wide", "narrow", None),
            P("wide", "narrow"),
            P("narrow", None),
            P("narrow", None),
            P(),
            P("wide", None),
        ),
        out_specs=(P("wide", "narrow"), P("narrow", None), P("narrow", None), P(None, "narrow")),
        check_vma=False,
    )
```

```python
import jax
import jax.numpy as jnp
from jax import lax
from jax.experimental import pallas as pl
from jax.experimental.pallas import tpu as pltpu
from jax.sharding import PartitionSpec as P

AXES = ("wide", "narrow")
NZ, NY, NC, NN = 8, 8, 2, 4
STEP = 8
VMEM = pl.BlockSpec(memory_space=pltpu.VMEM)
SMEM = pl.BlockSpec(memory_space=pltpu.SMEM)
ANY = pl.BlockSpec(memory_space=pl.ANY)
HBM = pl.BlockSpec(memory_space=pltpu.HBM)
F32, BF16, I32 = jnp.float32, jnp.bfloat16, jnp.int32
NEAR = (0, 6, 2, 7, 1)
FAR = (4, 5, 3)
RING = [(FAR if d in FAR else NEAR).index(d) * NZ * NN for d in range(NY)] + [int(d in FAR) for d in range(NY)]


def places():
    for z in range(NZ):
        for y in range(NY):
            for c in range(NC):
                for n in range(NN):
                    yield z, y, c, n


def device(z, y, c, n):
    return ((z * NY + y) * NC + c) * NN + n


def groups(key):
    found = {}
    for place in places():
        found.setdefault(key(*place), []).append(device(*place))
    return list(found.values())


FIRST = groups(lambda z, y, c, n: (0, y) if c == 0 else (1, z))
OVER_X = groups(lambda z, y, c, n: (z, y, c))
NEARBY = groups(lambda z, y, c, n: (z // 2, y // 2, n))
ALONG_Y = groups(lambda z, y, c, n: (z, y % 2, c, n))
ALONG_Z = groups(lambda z, y, c, n: (z % 2, y, c, n))
OTHER_CORE = [(device(z, y, c, n), device(z, y, 1 - c, n)) for z, y, c, n in places()]


def exchange(pieces, groups_):
    return lax.all_to_all(pieces, AXES, 0, 0, axis_index_groups=groups_, tiled=True)


def swap_cores(value):
    return lax.ppermute(value, AXES, OTHER_CORE)


def pass_on(value, even_hops, odd_hops):
    pairs = []
    for z, y, c, n in places():
        hops = odd_hops if (z if c else y) % 2 else even_hops
        to = (z, (y + hops) % NY, c, n) if c == 0 else ((z + hops) % NZ, y, c, n)
        pairs.append((device(z, y, c, n), device(*to)))
    return lax.ppermute(value, AXES, pairs)


def call(kernel, name, out_shape, in_specs, out_specs, scratch, vmem, flops, size, *args):
    return pl.pallas_call(
        kernel,
        out_shape=out_shape,
        in_specs=in_specs,
        out_specs=out_specs,
        scratch_shapes=scratch,
        compiler_params=pltpu.CompilerParams(vmem_limit_bytes=vmem << 20),
        cost_estimate=pl.CostEstimate(flops=flops, bytes_accessed=size, transcendentals=0),
        name=name,
    )(*args)


def place_kernel(where_ref, one_n_ref, own_ref, one_l_ref, meta_ref, order, tiles, sems):
    slots, half = own_ref.shape[0], own_ref.shape[2] // 2
    side = own_ref.shape[1]
    copies = [
        pltpu.make_async_copy(ref, tiles.at[k], sems.at[k]) for k, ref in enumerate((own_ref,))
    ]
    for copy in copies:
        copy.start()
    room = meta_ref.shape[1] - 2
    first = where_ref[0] == 0
    here = where_ref[1]
    low = lax.broadcasted_iota(I32, own_ref.shape[1:], 1) < half
    for block, (n_ref, l_ref) in enumerate(((one_n_ref, one_l_ref),)):
        count = n_ref[2 * slots]
        for k in range(room):
            order[k] = -1
            meta_ref[block, k] = 0

        def assign(s, carry, block=block, n_ref=n_ref):
            near, far = carry
            col = n_ref[slots + s]
            z, y = lax.shift_right_logical(col, 3), lax.bitwise_and(col, 7)
            ring = jnp.where(first, y, z)
            inner = jnp.where(first, z, y)
            away = lax.bitwise_and(ring - here + NY, NY - 1)
            is_far = where_ref[2 + NY + away]
            at = jnp.where(is_far == 1, room - 1 - far, near)
            order[at] = s
            meta_ref[block, at] = where_ref[2 + away] + inner * NN
            return near + 1 - is_far, far + is_far

        near, far = lax.fori_loop(0, count, assign, (jnp.int32(0), jnp.int32(0)))
        near_turns = lax.shift_right_logical(near + STEP - 1, 3)
        far_turns = lax.shift_right_logical(far + STEP - 1, 3)
        meta_ref[block, room] = near_turns
        meta_ref[block, room + 1] = room // STEP - far_turns

        def one_pair(p, carry, block=block, n_ref=n_ref, l_ref=l_ref):
            slot_a, slot_b = order[2 * p], order[2 * p + 1]
            at_a, at_b = jnp.maximum(slot_a, 0), jnp.maximum(slot_b, 0)
            a, b = tiles[block, at_a].astype(F32), tiles[block, at_b].astype(F32)
            moved = pltpu.roll(jnp.where(first, b, a), half, 1)
            both = jnp.where(low, jnp.where(first, a, moved), jnp.where(first, moved, b))
            row_a = jnp.where(slot_a >= 0, n_ref[at_a], -1)
            row_b = jnp.where(slot_b >= 0, n_ref[at_b], -1)
            rows = jnp.where(low, row_a, row_b)
            for r in range(2):
                l_ref[p, r * side:(r + 1) * side, :] = jnp.where(rows == r, both, 0.0).astype(BF16)
            return carry

        copies[block].wait()
        lax.fori_loop(0, near_turns * (STEP // 2), one_pair, 0)
        lax.fori_loop((room // STEP - far_turns) * (STEP // 2), room // 2, one_pair, 0)


def add_turns(meta_ref, block, first_turn, last_turn, l_ref, blocks, acc):
    def one_turn(i, carry):
        left = jnp.concatenate([l_ref[i * (STEP // 2) + k] for k in range(STEP // 2)], axis=1)
        spots = [meta_ref[block, i * STEP + k] for k in range(STEP)]
        right = jnp.concatenate(
            [jnp.concatenate([blocks[spot + n] for spot in spots], axis=0) for n in range(NN)],
            axis=1,
        )
        acc[...] += jnp.dot(left, right, preferred_element_type=F32)
        return carry

    lax.fori_loop(first_turn, last_turn, one_turn, 0)


def bring(refs, blocks, sems):
    copies, at = [], 0
    for k, ref in enumerate(refs):
        copies.append(
            pltpu.make_async_copy(ref, blocks.at[pl.ds(at, ref.shape[0])], sems.at[k])
        )
        at += ref.shape[0]
    for copy in copies:
        copy.start()
    return copies


def fetch(sources, targets, sems):
    copies = [
        pltpu.make_async_copy(source, target, sems.at[k])
        for k, (source, target) in enumerate(zip(sources, targets))
    ]
    for copy in copies:
        copy.start()
    return copies


def spread_kernel(f_from, out_ref, f_ref, sems):
    for copy in fetch((f_from,), (f_ref,), sems):
        copy.wait()
    quarter = out_ref.shape[1]
    for j in range(out_ref.shape[0]):
        out_ref[j] = f_ref[j % NN * quarter:(j % NN + 1) * quarter, :]


def pack_kernel(nw_from, rw_from, f_from, w_ref, nw_ref, rw_ref, f_ref, sems):
    for copy in fetch((nw_from, rw_from, f_from), (nw_ref, rw_ref, f_ref), sems):
        copy.wait()
    side = nw_ref.shape[0]
    quarter = f_ref.shape[0] // NN
    for j in range(NN):
        w_ref[j, :side, :] = nw_ref[...]
        w_ref[j, side:2 * side, :] = rw_ref[...]
        for q in range(NN):
            w_ref[j, 2 * side:, q * side:(q + 1) * side] = f_ref[q * quarter:(q + 1) * quarter, :]


def near_kernel(mo_ref, mt_ref, lo_ref, lt_ref, *refs):
    *given, po_ref, pt_ref, blocks, sems = refs
    room = mo_ref.shape[1] - 2
    copies = bring(given, blocks, sems)
    po_ref[...] = jnp.zeros_like(po_ref)
    pt_ref[...] = jnp.zeros_like(pt_ref)
    for copy in copies:
        copy.wait()
    add_turns(mt_ref, 0, 0, mt_ref[0, room], lt_ref, blocks, pt_ref)
    add_turns(mo_ref, 0, 0, mo_ref[0, room], lo_ref, blocks, po_ref)


def far_kernel(mo_ref, mt_ref, lo_ref, lt_ref, no_ref, nt_ref, *refs):
    *given, po_ref, pt_ref, acc, blocks, sems = refs
    room = mo_ref.shape[1] - 2
    copies = bring(given, blocks, sems)
    acc[...] = nt_ref[...]
    po_ref[...] = no_ref[...]
    for copy in copies:
        copy.wait()
    add_turns(mt_ref, 0, mt_ref[0, room + 1], room // STEP, lt_ref, blocks, acc)
    pt_ref[...] = acc[...].astype(BF16)
    add_turns(mo_ref, 0, mo_ref[0, room + 1], room // STEP, lo_ref, blocks, po_ref)


def join_kernel(own_ref, came_ref, out_ref):
    joined = (own_ref[...] + came_ref[...].astype(F32)).astype(BF16)
    for j in range(out_ref.shape[0]):
        out_ref[j] = joined


def total_kernel(in_ref, out_ref):
    summed = in_ref[0].astype(F32)
    for j in range(1, in_ref.shape[0]):
        summed = summed + in_ref[j].astype(F32)
    summed = summed.astype(BF16)
    for j in range(out_ref.shape[0]):
        out_ref[j] = summed


def last_kernel(in_ref, neighbor_ref, root_ref, output_ref):
    side = in_ref.shape[1]
    for j in range(NN):
        neighbor_ref[:, j * side:(j + 1) * side] = in_ref[j].astype(F32)
        root_ref[:, j * side:(j + 1) * side] = in_ref[NN + j].astype(F32)
        output_ref[j * side:(j + 1) * side, :] = in_ref[2 * NN + j].astype(F32)


def dense_kernel(n_ref, a_ref, w_ref, f_ref, cot_ref, ow_ref, out_ref, g_ref, agg_ref):
    side = f_ref.shape[1]
    quarter = w_ref.shape[1] - 2 * side
    mine = pl.ds(pl.multiple_of(n_ref[0] * side, side), side)
    root_weight = jnp.concatenate([w_ref[j, side:2 * side, :] for j in range(NN)], axis=0)
    neighbor_weight = jnp.concatenate([w_ref[j, :side, :] for j in range(NN)], axis=0)
    rows = jnp.concatenate(
        [
            jnp.concatenate(
                [w_ref[j, 2 * side:, q * side:(q + 1) * side] for j in range(NN)], axis=1
            )
            for q in range(NN)
        ],
        axis=0,
    )
    agg = a_ref[0].astype(F32)
    for j in range(1, NN):
        agg = agg + a_ref[j].astype(F32)
    agg = agg.astype(BF16)
    agg_ref[...] = agg
    pre = jnp.dot(agg, neighbor_weight, preferred_element_type=F32) + jnp.dot(
        rows, root_weight, preferred_element_type=F32
    )
    hidden_grad = lax.dot_general(
        cot_ref[...], ow_ref[...], (((1,), (1,)), ((), ())), preferred_element_type=F32
    )
    s = jax.nn.sigmoid(pre)
    hidden = (pre * s).astype(BF16)
    pre_grad = (hidden_grad * s * (1.0 + pre * (1.0 - s))).astype(BF16)
    over_rows = (((0,), (0,)), ((), ()))
    parts = (
        lax.dot_general(agg_ref[:, mine], pre_grad, over_rows, preferred_element_type=F32),
        lax.dot_general(f_ref[...], pre_grad, over_rows, preferred_element_type=F32),
    )
    for k, part in enumerate(parts):
        for j in range(NN):
            g_ref[k * NN + j] = part[:, j * side:(j + 1) * side].astype(BF16)
    part = lax.dot_general(hidden, cot_ref[:, mine], over_rows, preferred_element_type=F32)
    for j in range(NN):
        g_ref[2 * NN + j] = part[j * side:(j + 1) * side, :].astype(BF16)
    out_ref[...] = (
        f_ref[...].astype(F32) + jnp.dot(hidden, ow_ref[:, mine], preferred_element_type=F32)
    ).astype(BF16)


def per_device(
    features,
    tile_blocks,
    tile_rows,
    tile_cols,
    tile_count,
    neighbor_weight,
    root_weight,
    output_weight,
    cotangent,
):
    rows, side = features.shape
    width = NN * side
    quarter = rows // NN
    slots = tile_rows.shape[-1]
    wide = lax.axis_index("wide")
    narrow = lax.axis_index("narrow").astype(I32)
    core = wide % NC
    here = jnp.where(core == 0, (wide // NC) % NY, wide // (NC * NY))

    tiles = tile_blocks[0, 0]
    numbers = jnp.concatenate([tile_rows[0, 0], tile_cols[0, 0], tile_count[0]])
    other_tiles = swap_cores(tiles)
    other_numbers = swap_cores(numbers)

    pieces = call(
        spread_kernel,
        "spread",
        jax.ShapeDtypeStruct((NZ * NN, quarter, side), BF16),
        [HBM],
        VMEM,
        [pltpu.VMEM((rows, side), BF16), pltpu.SemaphoreType.DMA((1,))],
        56,
        10**5,
        10**6,
        features,
    )
    line = exchange(pieces, FIRST)

    weights = call(
        pack_kernel,
        "pack",
        jax.ShapeDtypeStruct((NN, 2 * side + quarter, width), BF16),
        [HBM, HBM, HBM],
        VMEM,
        [
            pltpu.VMEM((side, width), BF16),
            pltpu.VMEM((side, width), BF16),
            pltpu.VMEM((rows, side), BF16),
            pltpu.SemaphoreType.DMA((3,)),
        ],
        56,
        10**5,
        2 * 10**6,
        neighbor_weight,
        root_weight,
        features,
    )
    line, weights, other_numbers = lax.optimization_barrier((line, weights, other_numbers))
    all_weights = exchange(weights, OVER_X)
    by_distance = {0: line}
    for hops in (2, -2, 1, -1):
        by_distance[-hops % NY] = pass_on(line, hops, hops)
    where = jnp.concatenate([jnp.stack([core, here]).astype(I32), jnp.array(RING, I32)])
    turns = (slots + 2 * STEP - 2) // STEP
    placed = jax.ShapeDtypeStruct((turns * STEP // 2, rows, side), BF16)

    def place(of_numbers, of_tiles):
        return call(
            place_kernel,
            "place",
            (placed, jax.ShapeDtypeStruct((1, turns * STEP + 2), I32)),
            [SMEM, SMEM, ANY],
            (VMEM, SMEM),
            [
                pltpu.SMEM((turns * STEP,), I32),
                pltpu.VMEM((1, *tiles.shape), BF16),
                pltpu.SemaphoreType.DMA((1,)),
            ],
            8,
            10**7,
            4 * 10**6,
            where,
            of_numbers,
            of_tiles,
        )

    left_own, meta_own = place(numbers, tiles)
    left_other, meta_other = place(other_numbers, other_tiles)
    by_distance[2], by_distance[6], meta_own = lax.optimization_barrier(
        (by_distance[2], by_distance[6], meta_own)
    )
    across = jnp.where(here % 2 == 0, by_distance[2], by_distance[6])
    arrived, across = lax.optimization_barrier(([by_distance[d] for d in NEAR[1:3]], across))
    by_distance.update(zip(NEAR[1:3], arrived))
    for hops in (1, -1):
        by_distance[-3 * hops % NY] = pass_on(by_distance[-2 * hops % NY], hops, hops)
    by_distance[4] = pass_on(across, -2, 2)
    whole = jax.ShapeDtypeStruct((rows, width), F32)
    flops = 2 * slots * rows * quarter * width
    line_size = NZ * NN
    near_own, near_other = call(
        near_kernel,
        "near",
        (whole, whole),
        [SMEM, SMEM, VMEM, VMEM] + [ANY] * len(NEAR),
        (VMEM, VMEM),
        [
            pltpu.VMEM((len(NEAR) * line_size, quarter, side), BF16),
            pltpu.SemaphoreType.DMA((len(NEAR),)),
        ],
        20,
        flops,
        8 * 10**6,
        meta_own,
        meta_other,
        left_own,
        left_other,
        *[by_distance[d] for d in NEAR],
    )
    part_own, part_other = call(
        far_kernel,
        "far",
        (whole, jax.ShapeDtypeStruct((rows, width), BF16)),
        [SMEM, SMEM, VMEM, VMEM, VMEM, VMEM] + [ANY] * len(FAR),
        (VMEM, VMEM),
        [
            pltpu.VMEM((rows, width), F32),
            pltpu.VMEM((len(FAR) * line_size, quarter, side), BF16),
            pltpu.SemaphoreType.DMA((len(FAR),)),
        ],
        20,
        flops // 2,
        6 * 10**6,
        meta_own,
        meta_other,
        left_own,
        left_other,
        near_own,
        near_other,
        *[by_distance[d] for d in FAR],
    )
    copies = call(
        join_kernel,
        "join",
        jax.ShapeDtypeStruct((NN, rows, width), BF16),
        [VMEM, VMEM],
        VMEM,
        [],
        8,
        10**6,
        2 * 10**6,
        part_own,
        swap_cores(part_other),
    )
    parts = exchange(copies, OVER_X)

    layer_output, grads = call(
        dense_kernel,
        "dense",
        (
            jax.ShapeDtypeStruct((rows, side), BF16),
            jax.ShapeDtypeStruct((3 * NN, side, side), BF16),
        ),
        [SMEM] + [VMEM] * 5,
        (VMEM, VMEM),
        [pltpu.VMEM((rows, width), BF16)],
        16,
        12 * rows * width * width,
        5 * 10**6,
        narrow[None],
        parts,
        all_weights,
        features,
        cotangent,
        output_weight,
    )

    nearby = len(NEARBY[0])
    chunk = 3 * NN * side // nearby

    def total(pieces, count):
        return call(
            total_kernel,
            "total",
            jax.ShapeDtypeStruct((count, chunk, side), BF16),
            [VMEM],
            VMEM,
            [],
            4,
            10**6,
            10**6,
            pieces,
        )

    summed = total(exchange(grads.reshape(nearby, chunk, side), NEARBY), NY // 2)
    summed = total(exchange(summed, ALONG_Y), NZ // 2)
    summed = total(exchange(summed, ALONG_Z), nearby)
    full = exchange(summed, NEARBY).reshape(3 * NN, side, side)
    return layer_output, *call(
        last_kernel,
        "last",
        (
            jax.ShapeDtypeStruct((side, width), F32),
            jax.ShapeDtypeStruct((side, width), F32),
            jax.ShapeDtypeStruct((width, side), F32),
        ),
        [VMEM],
        (VMEM, VMEM, VMEM),
        [],
        4,
        10**6,
        10**6,
        full,
    )


def solution(mesh):
    return jax.shard_map(
        per_device,
        mesh=mesh,
        in_specs=(
            P("wide", "narrow"),
            P("wide", "narrow", None, None, None),
            P("wide", "narrow", None),
            P("wide", "narrow", None),
            P("wide", "narrow"),
            P("narrow", None),
            P("narrow", None),
            P(),
            P("wide", None),
        ),
        out_specs=(P("wide", "narrow"), P("narrow", None), P("narrow", None), P(None, "narrow")),
        check_vma=False,
    )
```
